32 devices in a mesh: band: 4 (over y, x), grp: 4 (over z), row: 2 (over core).
Axes of the slice: x: 2, y: 2, z: 4, core: 2. Of those that a mesh axis runs over, the one named last changes fastest.
Arguments:
- kspace_data: float32 [4, 16, 2, 2048], P('grp', 'row'), may hold values from -6 to 6
- coil_maps: bfloat16 [4, 4, 16, 256, 512], P('band', 'grp', 'row'), may hold values from -1.5 to 1.5
- smooth_weight: float32 [4, 4, 256, 256], P('band', 'grp', 'row'), may hold values from 0.3 to 3
- kernel_cols: bfloat16 [2048, 16], replicated, may hold values from -1.5 to 1.5
- kernel_rows: bfloat16 [2048, 16], replicated, may hold values from -1.5 to 1.5
- tile_index: int32 [16], replicated, may hold values from 0 to 255
- caipi_cycle: int32 [4], P('band'), may hold values from 0 to 3
Outputs:
- solution_field: float32 [4, 4, 256, 512], P('band', 'grp', 'row')
- residual: float32 [4, 4, 256, 512], P('band', 'grp', 'row')
The draws below stay inside these ranges and needn't reach their ends.
All inputs are finite; a program needn't handle non-finite values.
Results may differ from the reference program's by a relative error of at most 0.0003.
Values sent between devices are 32-bit elements; how exact they have to be, the bound alone decides.
No kernel may reach another device: no remote copies, remote signals or barrier semaphores. Data moves between devices by JAX's collectives and lax.ppermute only.
A program may use at most 128 MiB of HBM per device.

```python
import math
import jax
import jax.numpy as jnp
from jax import lax

NY = 256
NX = 256
COILS = 16
TY = 16
TX = 16
SB = 128
NBLK = 16
ITERS = 1
MB = 4
GROUPS = 4
NTILES = 256
SAMPLES = 2048


def draw_coil_maps(key, part):
    shape = (MB, GROUPS, COILS, NY, 2 * NX)
    row_place = jnp.arange(NY, dtype=jnp.float32) / (NY - 1)
    slice_place = jnp.arange(MB, dtype=jnp.float32) / max(MB - 1, 1)
    ramp = (0.5 + row_place)[None, None, None, :, None] * (0.6 + 0.8 * slice_place)[:, None, None, None, None]
    values = 0.25 * ramp * jax.random.normal(key, shape, jnp.float32)
    return jnp.clip(values, -1.5, 1.5).astype(jnp.bfloat16)


def draw_kspace_data(key, part):
    shape = (GROUPS, COILS, 2, SAMPLES)
    group_place = jnp.arange(GROUPS, dtype=jnp.float32) / max(GROUPS - 1, 1)
    ramp = (0.5 + group_place)[:, None, None, None]
    values = ramp * jax.random.normal(key, shape, jnp.float32)
    return jnp.clip(values, -6.0, 6.0)


def set_ends(entries, key, least, largest):
    shape = entries.shape
    place = [jax.random.randint(jax.random.fold_in(key, axis), (), 0, shape[axis]) for axis in range(len(shape))]
    entries = entries.at[tuple(place)].set(least)
    longest = shape.index(max(shape))
    place[longest] = (place[longest] + 1) % shape[longest]
    return entries.at[tuple(place)].set(largest)


def block_scale(key, dims, pieces, low, top_value):
    gain = 1.0
    for position, shards_of in pieces:
        draws = jax.random.uniform(jax.random.fold_in(jax.random.fold_in(key, 6), position), (shards_of,), jnp.float32, low / len(pieces), top_value / len(pieces))
        gain = gain * jnp.repeat(jnp.exp(draws), dims[position] // shards_of).reshape((-1,) + (1,) * (len(dims) - 1 - position))
    return gain


def normal_values(own_key, dims, scale, reach, held_as=jnp.bfloat16):
    return jnp.clip(scale * jax.random.normal(own_key, dims, jnp.float32), -reach, reach).astype(held_as)


def setup_inputs(seed: int = 0) -> dict:
    key_list = jax.random.split(jax.random.key(seed), 8)
    kspace_data = draw_kspace_data(jax.random.fold_in(key_list[7], 71), 0)
    coil_maps = draw_coil_maps(jax.random.fold_in(key_list[7], 71), 0)
    smooth_weight = jnp.clip(jnp.exp(math.log(3.0) - 2.3025851 * jax.random.uniform(key_list[2], (MB, GROUPS, NY, NX), jnp.float32) ** block_scale(key_list[2], (MB, GROUPS, NY, NX), ((0, 4), (1, 4), (2, 2)), -0.2, 0.2)), 0.3, 3.0)
    kernel_cols = normal_values(key_list[3], (SAMPLES, TX), TX ** -0.5, 1.5)
    kernel_rows = normal_values(key_list[4], (SAMPLES, TY), TY ** -0.5, 1.5)
    tile_index = set_ends(jax.random.randint(key_list[5], (NBLK,), 0, NTILES), jax.random.fold_in(key_list[5], 1), 0, NTILES - 1).astype(jnp.int32)
    caipi_cycle = set_ends(jax.random.randint(key_list[6], (MB,), 0, MB), jax.random.fold_in(key_list[6], 1), 0, MB - 1).astype(jnp.int32)
    return dict(kspace_data=kspace_data, coil_maps=coil_maps, smooth_weight=smooth_weight, kernel_cols=kernel_cols, kernel_rows=kernel_rows, tile_index=tile_index, caipi_cycle=caipi_cycle)


reg_strength = 0.5
damping = 1.0
two_pi = 6.283185307179586
highest = lax.Precision.HIGHEST


def to_tiles(grid):
    count = grid.shape[0]
    shaped = grid.reshape(count, NY // TY, TY, 2, NX // TX, TX)
    return shaped.transpose(1, 4, 0, 3, 2, 5).reshape(NTILES, count * 2, TY, TX)


def from_tiles(tiles, count):
    shaped = tiles.reshape(NY // TY, NX // TX, count, 2, TY, TX)
    return shaped.transpose(2, 0, 4, 3, 1, 5).reshape(count, NY, 2 * NX)


def coil_images(profiles, image):
    profile = profiles.astype(jnp.float32)
    width = image.shape[-1] // 2
    coil_real, coil_imag = profile[..., :width], profile[..., width:]
    image_real, image_imag = image[None, :, :width], image[None, :, width:]
    return jnp.concatenate([coil_real * image_real - coil_imag * image_imag, coil_real * image_imag + coil_imag * image_real], axis=-1)


def combine_coils(profiles, images):
    profile = profiles.astype(jnp.float32)
    width = images.shape[-1] // 2
    coil_real, coil_imag = profile[..., :width], profile[..., width:]
    image_real, image_imag = images[..., :width], images[..., width:]
    real_sum = jnp.sum(coil_real * image_real + coil_imag * image_imag, axis=0)
    imag_sum = jnp.sum(coil_real * image_imag - coil_imag * image_real, axis=0)
    return jnp.concatenate([real_sum, imag_sum], axis=-1)


def to_complex(values):
    width = values.shape[-1] // 2
    return lax.complex(values[..., :width], values[..., width:])


def from_complex(values):
    return jnp.concatenate([jnp.real(values), jnp.imag(values)], axis=-1)


def sample_blocks(tiles, tile_index, kernel_cols, kernel_rows):
    picked = jnp.take(tiles, tile_index, axis=0)
    col_weight = kernel_cols.astype(jnp.float32).reshape(NBLK, SB, TX)
    row_weight = kernel_rows.astype(jnp.float32).reshape(NBLK, SB, TY)
    partial_sum = jnp.einsum("bcyx,bsx->bcys", picked, col_weight, precision=highest)
    return jnp.einsum("bcys,bsy->bcs", partial_sum, row_weight, precision=highest)


def spread_blocks(values, kernel_cols, kernel_rows):
    col_weight = kernel_cols.astype(jnp.float32).reshape(NBLK, SB, TX)
    row_weight = kernel_rows.astype(jnp.float32).reshape(NBLK, SB, TY)
    partial_sum = jnp.einsum("bcs,bsy->bcys", values, row_weight, precision=highest)
    return jnp.einsum("bcys,bsx->bcyx", partial_sum, col_weight, precision=highest)


def forward_slice(image, profiles, phase_cos, phase_sin, tile_index, kernel_cols, kernel_rows):
    coils = coil_images(profiles, image)
    grid = from_complex(jnp.fft.fft2(to_complex(coils), norm="ortho"))
    predicted = sample_blocks(to_tiles(grid), tile_index, kernel_cols, kernel_rows)
    predicted = predicted.reshape(NBLK, COILS, 2, SB)
    real_part, imag_part = predicted[:, :, 0], predicted[:, :, 1]
    cosine, sine = phase_cos[:, None, None], phase_sin[:, None, None]
    turned = jnp.stack([cosine * real_part - sine * imag_part, sine * real_part + cosine * imag_part], axis=2)
    return turned.transpose(1, 2, 0, 3).reshape(COILS, 2, SAMPLES)


def adjoint_slice(kspace, profiles, phase_cos, phase_sin, tile_index, kernel_cols, kernel_rows):
    shaped = kspace.reshape(COILS, 2, NBLK, SB)
    real_part, imag_part = shaped[:, 0], shaped[:, 1]
    cosine, sine = phase_cos[None, :, None], phase_sin[None, :, None]
    back = jnp.stack([cosine * real_part + sine * imag_part, cosine * imag_part - sine * real_part], axis=1)
    values = back.transpose(2, 0, 1, 3).reshape(NBLK, COILS * 2, SB)
    spread = spread_blocks(values, kernel_cols, kernel_rows)
    summed = jax.ops.segment_sum(spread, tile_index, num_segments=NTILES)
    grid = from_tiles(summed, COILS)
    image = from_complex(jnp.fft.ifft2(to_complex(grid), norm="ortho"))
    return combine_coils(profiles, image)


def phases(caipi_cycle):
    blocks = jnp.arange(NBLK, dtype=jnp.int32)
    turns = (caipi_cycle[:, None] * blocks[None, :]) % MB
    angle = turns.astype(jnp.float32) * (two_pi / MB)
    return jnp.cos(angle), jnp.sin(angle)


def edge_term(values, weights, axis):
    count = values.shape[axis]
    diff = lax.slice_in_dim(values, 0, count - 1, axis=axis) - lax.slice_in_dim(values, 1, count, axis=axis)
    coupling = lax.slice_in_dim(weights, 0, count - 1, axis=axis) * lax.slice_in_dim(weights, 1, count, axis=axis)
    flux = coupling * diff
    after = [(0, 0)] * values.ndim
    before = [(0, 0)] * values.ndim
    after[axis] = (0, 1)
    before[axis] = (1, 0)
    return jnp.pad(flux, after) - jnp.pad(flux, before)


def laplace(images, weights):
    doubled = jnp.concatenate([weights, weights], axis=-1)
    total = edge_term(images, doubled, 1) + edge_term(images, doubled, 2)
    shaped = images.reshape(images.shape[:-1] + (2, NX))
    columns = edge_term(shaped, weights[..., None, :], shaped.ndim - 1)
    return total + columns.reshape(images.shape)


def reference(kspace_data, coil_maps, smooth_weight, kernel_cols, kernel_rows, tile_index, caipi_cycle):
    phase_cos, phase_sin = phases(caipi_cycle)
    flat_cos = jnp.repeat(phase_cos, GROUPS, axis=0)
    flat_sin = jnp.repeat(phase_sin, GROUPS, axis=0)
    flat_maps = coil_maps.reshape(MB * GROUPS, COILS, NY, 2 * NX)

    def forward_one(inputs):
        image, profiles, cosine, sine = inputs
        return forward_slice(image, profiles, cosine, sine, tile_index, kernel_cols, kernel_rows)

    def adjoint_one(inputs):
        kspace, profiles, cosine, sine = inputs
        return adjoint_slice(kspace, profiles, cosine, sine, tile_index, kernel_cols, kernel_rows)

    def forward_all(images):
        flat_images = images.reshape(MB * GROUPS, NY, 2 * NX)
        predicted = lax.map(forward_one, (flat_images, flat_maps, flat_cos, flat_sin))
        return jnp.sum(predicted.reshape(MB, GROUPS, COILS, 2, SAMPLES), axis=0)

    def adjoint_all(collapsed):
        spread = jnp.broadcast_to(collapsed[None], (MB,) + collapsed.shape).reshape(MB * GROUPS, COILS, 2, SAMPLES)
        images = lax.map(adjoint_one, (spread, flat_maps, flat_cos, flat_sin))
        return images.reshape(MB, GROUPS, NY, 2 * NX)

    def apply_normal(direction):
        return adjoint_all(forward_all(direction)) + reg_strength * laplace(direction, smooth_weight) + damping * direction

    rhs = adjoint_all(kspace_data)
    solution_field = jnp.zeros_like(rhs)
    residual = rhs
    direction = rhs
    norm_now = jnp.sum(residual * residual)
    for step in range(ITERS):
        image = apply_normal(direction)
        alpha = norm_now / jnp.sum(direction * image)
        solution_field = solution_field + alpha * direction
        residual = residual - alpha * image
        norm_next = jnp.sum(residual * residual)
        direction = residual + (norm_next / norm_now) * direction
        norm_now = norm_next
    return solution_field, residual
```

```python
import functools
import math

import jax
import jax.numpy as jnp
import ml_dtypes
import numpy as np
from jax import lax
from jax.experimental import pallas as pl
from jax.experimental.pallas import tpu as pltpu
from jax.sharding import PartitionSpec as P

reg_strength = 0.5
damping = 1.0
f32 = jnp.float32
bf16 = jnp.bfloat16
VMEM = pl.BlockSpec(memory_space=pltpu.VMEM)
SMEM = pl.BlockSpec(memory_space=pltpu.SMEM)
HBM = pl.BlockSpec(memory_space=pltpu.HBM)
TN = (((0,), (0,)), ((), ()))
NT = (((1,), (1,)), ((), ()))
large_vmem = 20 * 1024 * 1024
small_vmem = 8 * 1024 * 1024


def dft_table(length):
    index = np.arange(length)
    angle = (index[:, None] * index[None, :] % length) * (2.0 * np.pi / length)
    parts = []
    for part in (np.cos(angle) / math.sqrt(length), -np.sin(angle) / math.sqrt(length)):
        high = part.astype(ml_dtypes.bfloat16)
        low = (part - high.astype(np.float64)).astype(ml_dtypes.bfloat16)
        parts += [high, low]
    return np.concatenate(parts, axis=0)


def split(values):
    high = values.astype(bf16)
    return high, (values - high.astype(f32)).astype(bf16)


def matmul(left, right):
    return jnp.dot(left, right, preferred_element_type=f32)


def quarter_turn(cycle, block):
    turn = lax.rem(cycle * block, 4)
    one, zero = jnp.float32(1.0), jnp.float32(0.0)
    cosine = jnp.where(turn == 0, one, zero) - jnp.where(turn == 2, one, zero)
    sine = jnp.where(turn == 1, one, zero) - jnp.where(turn == 3, one, zero)
    return cosine, sine


def spread(values, row_weight, whigh, wlow, xhigh, xlow, k, coils, ty):
    weighted = values[:, None, :] * row_weight[None, :, :]
    parts = split(weighted.reshape(coils * ty, values.shape[1]))
    sb = values.shape[1] // 2
    vhigh, vlow = (
        jnp.concatenate([part, jnp.concatenate([part[:, sb:], -part[:, :sb]], axis=1)], axis=0) for part in parts
    )
    rows = matmul(
        jnp.concatenate([vhigh, vlow, vhigh], axis=1),
        jnp.concatenate([whigh, whigh, wlow], axis=0),
    )
    high, low = split(rows)
    half = xhigh.shape[1] // 2
    for part in range(2):
        there = pl.ds(part * half + k * ty, ty)
        for c in range(coils):
            here = slice((part * coils + c) * ty, (part * coils + c + 1) * ty)
            xhigh[c, there, :] = high[here]
            xlow[c, there, :] = low[here]


def back_rows(table, xhigh, xlow, coil, coils, out_rows):
    nx = xhigh.shape[2]
    real_sum = imag_sum = None
    for c in range(coils):
        high, low = xhigh[c], xlow[c]
        image = matmul(table, jnp.concatenate([high, high, low], axis=0))
        real, imag = image[:out_rows], image[out_rows:]
        coil_real = coil[c, :, :nx].astype(f32)
        coil_imag = coil[c, :, nx:].astype(f32)
        real_term = coil_real * real + coil_imag * imag
        imag_term = coil_real * imag - coil_imag * real
        real_sum = real_term if c == 0 else real_sum + real_term
        imag_sum = imag_term if c == 0 else imag_sum + imag_term
    return real_sum, imag_sum


def rhs_kernel(
    coils, blocks, place_ref, tile_ref, cycle_ref, table_ref, cols_ref, rows_ref, data_ref, weight_ref, coil_any,
    part_ref, whigh, wlow, adj, row_weight_ref, coil, xhigh, xlow, sem,
):
    ny = table_ref.shape[1]
    ty, tx = rows_ref.shape[0], cols_ref.shape[0]
    sb = rows_ref.shape[1] // blocks
    width = blocks * ty
    fetch = pltpu.make_async_copy(coil_any, coil, sem)
    fetch.start()

    lane = lax.broadcasted_iota(jnp.int32, (ny, width), 1)
    wanted = lax.rem(lane, ty)
    for k in range(blocks):
        first = (tile_ref[k] // (ny // tx)) * ty
        wanted = wanted + jnp.where(lane // ty == k, first, 0)
    pick = (lax.broadcasted_iota(jnp.int32, (ny, width), 0) == wanted).astype(f32).astype(bf16)
    picked = matmul(table_ref[...], pick).astype(bf16)
    real_high, real_low, imag_high, imag_low = (picked[i * ny : (i + 1) * ny] for i in range(4))
    high = jnp.concatenate(
        [jnp.concatenate([real_high, imag_high], axis=1), jnp.concatenate([-imag_high, real_high], axis=1)], axis=0
    )
    low = jnp.concatenate(
        [jnp.concatenate([real_low, imag_low], axis=1), jnp.concatenate([-imag_low, real_low], axis=1)], axis=0
    )
    adj[:, : 2 * width] = high
    adj[:, 2 * width : 4 * width] = low
    adj[:, 4 * width :] = high

    for k in range(blocks):
        left = pl.multiple_of(lax.rem(tile_ref[k], ny // tx) * tx, tx)
        chosen = [table_ref[pl.ds(i * ny + left, tx), :] for i in range(4)]
        stacked = jnp.concatenate(
            [jnp.concatenate([chosen[0], chosen[2]], axis=1), jnp.concatenate([chosen[1], chosen[3]], axis=1)], axis=0
        )
        here = slice(k * sb, (k + 1) * sb)
        cols = cols_ref[:, here]
        mixed = lax.dot_general(
            jnp.concatenate([cols, cols], axis=0), stacked, TN, preferred_element_type=f32
        )
        for ref, part in zip((whigh, wlow), split(mixed)):
            ref[k, :sb, :] = part[:, :ny]
            ref[k, sb:, :] = part[:, ny:]
        turned = rows_ref[:, here].astype(f32)
        row_weight = jnp.concatenate([turned, turned], axis=1)
        row_weight_ref[k] = row_weight
        cosine, sine = quarter_turn(cycle_ref[0], k)
        real, imag = data_ref[:, 0, here], data_ref[:, 1, here]
        values = jnp.concatenate([cosine * real + sine * imag, cosine * imag - sine * real], axis=1)
        spread(values, row_weight, whigh[k], wlow[k], xhigh, xlow, k, coils, ty)

    fetch.wait()
    real_sum, imag_sum = back_rows(adj[...], xhigh, xlow, coil, coils, ny)
    part_ref[:ny, :] = jnp.concatenate([real_sum, imag_sum], axis=1)
    count = weight_ref.shape[0]
    edge = jnp.concatenate([weight_ref[0:1, :], weight_ref[count - 1 : count, :]], axis=0)
    edge = jnp.concatenate([edge, jnp.zeros((6, edge.shape[1]), f32)], axis=0)
    part_ref[ny:, :] = jnp.concatenate([edge, jnp.zeros_like(edge)], axis=1)


def sum_kernel(ny, count, place_ref, weight_ref, *refs):
    parts, (image_ref, packed_ref) = refs[:-2], refs[-2:]
    total = parts[0][:ny, :]
    for part in parts[1:]:
        total = total + part[:ny, :]
    image_ref[...] = total
    start = pl.multiple_of(place_ref[0] * count, count)
    width = total.shape[1]
    packed_ref[:, :width] = image_ref[pl.ds(start, count), :]
    packed_ref[:, width:] = weight_ref[...]


def predict_kernel(
    coils, blocks, tile_ref, cycle_ref, table_ref, row_weight_ref, image_ref, coil, whigh, wlow,
    out_ref, fwd, thigh, tlow,
):
    ny = table_ref.shape[1]
    nx = image_ref.shape[1] // 2
    ty = row_weight_ref.shape[1]
    sb = row_weight_ref.shape[2] // 2
    width = blocks * ty
    for k in range(blocks):
        top = pl.multiple_of((tile_ref[k] // (nx // ty)) * ty, ty)
        real_high, real_low, imag_high, imag_low = (table_ref[pl.ds(i * ny + top, ty), :] for i in range(4))
        upper, lower = slice(k * ty, (k + 1) * ty), slice(width + k * ty, width + (k + 1) * ty)
        for place, real, imag in ((0, real_high, imag_high), (2, real_low, imag_low), (4, real_high, imag_high)):
            fwd[upper, place * ny : (place + 1) * ny] = real
            fwd[upper, (place + 1) * ny : (place + 2) * ny] = -imag
            fwd[lower, place * ny : (place + 1) * ny] = imag
            fwd[lower, (place + 1) * ny : (place + 2) * ny] = real
    image_real, image_imag = image_ref[:, :nx], image_ref[:, nx:]
    for c in range(coils):
        coil_real = coil[c, :, :nx].astype(f32)
        coil_imag = coil[c, :, nx:].astype(f32)
        product = jnp.concatenate(
            [coil_real * image_real - coil_imag * image_imag, coil_real * image_imag + coil_imag * image_real], axis=0
        )
        high, low = split(product)
        grid = matmul(fwd[...], jnp.concatenate([high, high, low], axis=0))
        for ref, part in zip((thigh, tlow), split(grid)):
            ref[:, 0, c * ty : (c + 1) * ty, :] = part[:width].reshape(blocks, ty, nx)
            ref[:, 1, c * ty : (c + 1) * ty, :] = part[width:].reshape(blocks, ty, nx)
    for k in range(blocks):
        left_high, left_low = (ref[k].reshape(2 * coils * ty, nx) for ref in (thigh, tlow))
        right_high = whigh[k]
        mixed = lax.dot_general(
            jnp.concatenate([left_high, left_low, left_high], axis=1),
            jnp.concatenate([right_high, right_high, wlow[k]], axis=1),
            NT,
            preferred_element_type=f32,
        )
        of_real, of_imag = mixed[: coils * ty], mixed[coils * ty :]
        product = jnp.concatenate(
            [of_real[:, :sb] - of_imag[:, sb:], of_real[:, sb:] + of_imag[:, :sb]], axis=1
        )
        summed = jnp.sum(product.reshape(coils, ty, 2 * sb) * row_weight_ref[k][None, :, :], axis=1)
        real, imag = summed[:, :sb], summed[:, sb:]
        cosine, sine = quarter_turn(cycle_ref[0], k)
        out_ref[k] = jnp.concatenate([cosine * real - sine * imag, sine * real + cosine * imag], axis=1)


def image_kernel(
    coils, blocks, place_ref, cycle_ref, row_weight_ref, collapsed_ref, adj, coil, whigh, wlow, *refs,
):
    *out_refs, whole, xhigh, xlow = refs
    ty = row_weight_ref.shape[1]
    sb = row_weight_ref.shape[2] // 2
    for k in range(blocks):
        cosine, sine = quarter_turn(cycle_ref[0], k)
        real, imag = collapsed_ref[k, :, :sb], collapsed_ref[k, :, sb:]
        values = jnp.concatenate([cosine * real + sine * imag, cosine * imag - sine * real], axis=1)
        spread(values, row_weight_ref[k], whigh[k], wlow[k], xhigh, xlow, k, coils, ty)
    real_sum, imag_sum = back_rows(adj[...], xhigh, xlow, coil, coils, whole.shape[0])
    whole[...] = jnp.concatenate([real_sum, imag_sum], axis=1)
    for shift, out_ref in enumerate(out_refs):
        count = out_ref.shape[0]
        start = lax.rem(place_ref[0] + shift, whole.shape[0] // count) * count
        out_ref[...] = whole[pl.ds(pl.multiple_of(start, count), count), :]


def smooth_kernel(place_ref, image_ref, own_ref, low_ref, high_ref, before_ref, after_ref, out_ref, sums_ref):
    count = own_ref.shape[0]
    width = image_ref.shape[1]
    nx = width // 2
    place, places = place_ref[0], place_ref[1]
    total_rows = image_ref.shape[0]
    start = place * count
    weight = own_ref[:, width:]
    none = jnp.zeros((1, nx), f32)
    weight_up = jnp.where(place > 0, before_ref[total_rows + 1 : total_rows + 2, :nx], none)
    weight_down = jnp.where(place < places - 1, after_ref[total_rows : total_rows + 1, :nx], none)
    image_up = image_ref[pl.ds(jnp.maximum(start - 1, 0), 1), :]
    image_down = image_ref[pl.ds(jnp.minimum(start + count, total_rows - 1), 1), :]
    row = lax.broadcasted_iota(jnp.int32, (count, nx), 0)
    column = lax.broadcasted_iota(jnp.int32, (count, nx), 1)

    def above(values, edge):
        return jnp.where(row == 0, edge, pltpu.roll(values, 1, 0))

    def below(values, edge):
        return jnp.where(row == count - 1, edge, pltpu.roll(values, count - 1, 0))

    weight_left = jnp.where(column == 0, 0.0, pltpu.roll(weight, 1, 1))
    weight_right = jnp.where(column == nx - 1, 0.0, pltpu.roll(weight, nx - 1, 1))
    weight_above, weight_below = above(weight, weight_up), below(weight, weight_down)
    weight_low, weight_high = low_ref[:, width:], high_ref[:, width:]
    squares = curvature = 0.0
    for part in range(2):
        lanes = slice(part * nx, (part + 1) * nx)
        here = own_ref[:, lanes]
        flux = weight_low * (here - low_ref[:, lanes]) + weight_high * (here - high_ref[:, lanes])
        flux += weight_above * (here - above(here, image_up[:, lanes]))
        flux += weight_below * (here - below(here, image_down[:, lanes]))
        flux += weight_left * (here - pltpu.roll(here, 1, 1))
        flux += weight_right * (here - pltpu.roll(here, nx - 1, 1))
        result = reg_strength * (weight * flux) + damping * here
        out_ref[:, lanes] = result
        squares += jnp.sum(here * here)
        curvature += jnp.sum(here * result)
    lane = lax.broadcasted_iota(jnp.int32, sums_ref.shape, 1)
    sums_ref[...] = jnp.where(lane == 0, squares, jnp.where(lane == 1, curvature, 0.0))


def collapse_kernel(sums_ref, *refs):
    parts, (out_ref, out_sums_ref) = refs[:-2], refs[-2:]
    total = parts[0][...]
    for part in parts[1:]:
        total = total + part[...]
    out_ref[...] = total
    lane = lax.broadcasted_iota(jnp.int32, sums_ref.shape, 1)
    out_sums_ref[...] = sums_ref[...] + jnp.where(lane == 1, jnp.sum(total * total), 0.0)


def call(kernel, outs, specs, out_specs, scratch=(), flops=0, nbytes=0, limit=small_vmem):
    return pl.pallas_call(
        kernel,
        out_shape=outs,
        in_specs=specs,
        out_specs=out_specs,
        scratch_shapes=scratch,
        compiler_params=pltpu.CompilerParams(vmem_limit_bytes=limit),
        cost_estimate=pl.CostEstimate(flops=flops, bytes_accessed=nbytes, transcendentals=0),
    )


def shape(dims, dtype=f32):
    return jax.ShapeDtypeStruct(dims, dtype)


def sum_over(values, axes):
    for axis in axes:
        count = lax.axis_size(axis)
        step = 1
        if count & (count - 1):
            values = lax.psum(values, axis)
            continue
        while step < count:
            values = values + lax.ppermute(values, axis, [(i, i ^ step) for i in range(count)])
            step *= 2
    return values


def from_others(values, axis):
    count = lax.axis_size(axis)
    return [
        lax.ppermute(values, axis, [(i, (i + shift) % count) for i in range(count)]) for shift in range(1, count)
    ]


def on_device(kspace_data, coil_maps, smooth_weight, kernel_cols, kernel_rows, tile_index, caipi_cycle):
    profiles, data, weight = coil_maps[0, 0], kspace_data[0], smooth_weight[0, 0]
    coils, ny, width = profiles.shape
    nx = width // 2
    blocks = tile_index.shape[0]
    samples, ty = kernel_rows.shape
    sb = samples // blocks
    count = weight.shape[0]
    bands, rows, groups = lax.axis_size("band"), lax.axis_size("row"), lax.axis_size("grp")
    row_place = lax.axis_index("row")
    table = jnp.asarray(dft_table(ny))
    wide = blocks * ty
    w_shape = (blocks, 2 * sb, nx)
    row_flops = 2 * 3 * coils * (2 * wide) * (2 * ny) * nx
    col_flops = 2 * 3 * coils * ty * blocks * (2 * sb) * width
    place = jnp.stack([row_place, jnp.int32(rows)])
    dma = pltpu.SemaphoreType.DMA
    x_scratch = [pltpu.VMEM((coils, 2 * wide, nx), bf16)] * 2

    data, weight, profiles, cols, rows_of, tile_index = (
        pltpu.with_memory_space_constraint(x, pltpu.HBM)
        for x in (data, weight, profiles, kernel_cols.T, kernel_rows.T, tile_index)
    )
    partial, *kept = call(
        functools.partial(rhs_kernel, coils, blocks),
        [
            shape((ny + 8, width)),
            pltpu.VMEM(w_shape, bf16),
            pltpu.VMEM(w_shape, bf16),
            pltpu.VMEM((2 * ny, 6 * wide), bf16),
            pltpu.VMEM((blocks, ty, 2 * sb), f32),
            pltpu.VMEM(profiles.shape, bf16),
        ],
        [SMEM, SMEM, SMEM, VMEM, VMEM, VMEM, VMEM, VMEM, HBM],
        [VMEM] * 6,
        [*x_scratch, dma],
        row_flops + 2 * col_flops,
        limit=large_vmem,
    )(place, tile_index, caipi_cycle, table, cols, rows_of, data, weight, profiles)

    whigh, wlow, adj, row_weight, coil = (pltpu.with_memory_space_constraint(x, pltpu.VMEM) for x in kept)

    received = from_others(partial, "row")
    image, packed = call(
        functools.partial(sum_kernel, ny, count),
        [shape((ny, width)), shape((count, width + nx))],
        [SMEM] + [VMEM] * (2 + len(received)),
        [VMEM, VMEM],
    )(place, weight, partial, *received)

    low = lax.ppermute(packed, "grp", [(i, i + 1) for i in range(groups - 1)])
    high = lax.ppermute(packed, "grp", [(i + 1, i) for i in range(groups - 1)])

    predicted = call(
        functools.partial(predict_kernel, coils, blocks),
        shape((blocks, coils, 2 * sb)),
        [SMEM, SMEM] + [VMEM] * 6,
        VMEM,
        [
            pltpu.VMEM((2 * wide, 6 * ny), bf16),
            *[pltpu.VMEM((blocks, 2, coils * ty, nx), bf16)] * 2,
        ],
        row_flops + col_flops,
        limit=large_vmem,
    )(tile_index, caipi_cycle, table, row_weight, image, coil, whigh, wlow)

    others = from_others(predicted, "band")
    smoothed, sums = call(
        smooth_kernel,
        [shape((count, width)), shape((8, 128))],
        [SMEM] + [VMEM] * 6,
        [VMEM, VMEM],
    )(place, image, packed, low, high, received[0], received[-1])
    sums = sum_over(sums, ("band",))
    collapsed, sums = call(
        collapse_kernel,
        [shape(predicted.shape), shape((8, 128))],
        [VMEM] * (2 + len(others)),
        [VMEM, VMEM],
    )(sums, predicted, *others)

    halves = call(
        functools.partial(image_kernel, coils, blocks),
        [shape((count, width))] * 2 if rows == 2 else [shape((ny, width))],
        [SMEM, SMEM] + [VMEM] * 6,
        [VMEM] * (2 if rows == 2 else 1),
        [pltpu.VMEM((ny, width), f32), *x_scratch],
        row_flops + col_flops,
        limit=large_vmem,
    )(place, caipi_cycle, row_weight, collapsed, adj, coil, whigh, wlow)
    sums = sum_over(sums, ("row", "grp"))

    if rows == 2:
        normal = halves[0] + lax.ppermute(halves[1], "row", [(0, 1), (1, 0)])
    else:
        normal = lax.psum_scatter(halves[0], "row", scatter_dimension=0, tiled=True)
    alpha = sums[0, 0] / sums[0, 1]
    direction = packed[:, :width]
    solution_field = alpha * direction
    residual = direction - alpha * (normal + smoothed)
    return solution_field[None, None], residual[None, None]


def solution(mesh):
    return jax.shard_map(
        on_device,
        mesh=mesh,
        in_specs=(
            P("grp", "row", None, None),
            P("band", "grp", "row", None, None),
            P("band", "grp", "row", None),
            P(),
            P(),
            P(),
            P("band"),
        ),
        out_specs=(P("band", "grp", "row", None), P("band", "grp", "row", None)),
        check_vma=False,
    )
```

```python
import functools
import math

import jax
import jax.numpy as jnp
import ml_dtypes
import numpy as np
from jax import lax
from jax.experimental import pallas as pl
from jax.experimental.pallas import tpu as pltpu
from jax.sharding import PartitionSpec as P

reg_strength = 0.5
damping = 1.0
f32 = jnp.float32
bf16 = jnp.bfloat16
VMEM = pl.BlockSpec(memory_space=pltpu.VMEM)
SMEM = pl.BlockSpec(memory_space=pltpu.SMEM)
HBM = pl.BlockSpec(memory_space=pltpu.HBM)
TN = (((0,), (0,)), ((), ()))
NT = (((1,), (1,)), ((), ()))
large_vmem = 20 * 1024 * 1024
small_vmem = 8 * 1024 * 1024


def dft_table(length):
    index = np.arange(length)
    angle = (index[:, None] * index[None, :] % length) * (2.0 * np.pi / length)
    parts = []
    for part in (np.cos(angle) / math.sqrt(length), -np.sin(angle) / math.sqrt(length)):
        high = part.astype(ml_dtypes.bfloat16)
        low = (part - high.astype(np.float64)).astype(ml_dtypes.bfloat16)
        parts += [high, low]
    return np.concatenate(parts, axis=0)


def split(values):
    high = values.astype(bf16)
    return high, (values - high.astype(f32)).astype(bf16)


def matmul(left, right):
    return jnp.dot(left, right, preferred_element_type=f32)


def quarter_turn(cycle, block):
    turn = lax.rem(cycle * block, 4)
    one, zero = jnp.float32(1.0), jnp.float32(0.0)
    cosine = jnp.where(turn == 0, one, zero) - jnp.where(turn == 2, one, zero)
    sine = jnp.where(turn == 1, one, zero) - jnp.where(turn == 3, one, zero)
    return cosine, sine


def spread(values, row_weight, whigh, wlow, xhigh, xlow, k, coils, ty):
    weighted = values[:, None, :] * row_weight[None, :, :]
    parts = split(weighted.reshape(coils * ty, values.shape[1]))
    sb = values.shape[1] // 2
    vhigh, vlow = (
        jnp.concatenate([part, jnp.concatenate([part[:, sb:], -part[:, :sb]], axis=1)], axis=0) for part in parts
    )
    rows = matmul(
        jnp.concatenate([vhigh, vlow, vhigh], axis=1),
        jnp.concatenate([whigh, whigh, wlow], axis=0),
    )
    high, low = split(rows)
    there, nx = slice(k * ty, (k + 1) * ty), rows.shape[1]
    for part in range(2):
        for c in range(coils):
            here = slice((part * coils + c) * ty, (part * coils + c + 1) * ty)
            xhigh[c, there, part * nx : (part + 1) * nx] = high[here]
            xlow[c, there, part * nx : (part + 1) * nx] = low[here]


def mirror(rows):
    left = lax.broadcasted_iota(jnp.int32, (rows, rows), 0)
    right = lax.broadcasted_iota(jnp.int32, (rows, rows), 1)
    return (lax.rem(left + right, rows) == 0).astype(f32).astype(bf16)


def mirrored(values):
    high, rest = split(values)
    low = (values - high.astype(f32) - rest.astype(f32)).astype(bf16)
    order = mirror(values.shape[0])
    return matmul(order, high) + (matmul(order, rest) + matmul(order, low))


def first_row(rows, columns):
    return lax.broadcasted_iota(jnp.int32, (rows, columns), 0) == 0


def back_rows(adj, xhigh, xlow, coil, first, last):
    ny, nx = adj.shape[0], xhigh.shape[2] // 2
    half = ny // 2
    edge = first_row(half, nx)
    sums = [None] * 4
    for c in range(first, last):
        high, low = xhigh[c], xlow[c]
        folded = matmul(adj[...], jnp.concatenate([high, high, low], axis=0))
        even_real, even_imag = folded[:half, :nx], folded[:half, nx:]
        odd_real, odd_imag = folded[half:, :nx], folded[half:, nx:]
        lower = even_real - jnp.where(edge, 0.0, odd_imag), even_imag + jnp.where(edge, 0.0, odd_real)
        upper = jnp.where(edge, odd_real, even_real + odd_imag), jnp.where(edge, odd_imag, even_imag - odd_real)
        for i, (real, imag) in enumerate((lower, upper)):
            here = slice(i * half, (i + 1) * half)
            coil_real = coil[c, here, :nx].astype(f32)
            coil_imag = coil[c, here, nx:].astype(f32)
            terms = coil_real * real + coil_imag * imag, coil_real * imag - coil_imag * real
            for j, term in enumerate(terms):
                sums[2 * i + j] = term if c == first else sums[2 * i + j] + term
    return jnp.concatenate(sums[:2], axis=1), jnp.concatenate(sums[2:], axis=1)


def rhs_kernel(
    coils, blocks, place_ref, tile_ref, cycle_ref, table_ref, cols_ref, rows_ref, data_ref, weight_ref, coil_any,
    part_ref, whigh, wlow, fwd, adj, row_weight_ref, coil, kept_ref, xhigh, xlow, upper, sems,
):
    ny = table_ref.shape[1]
    half = ny // 2
    ty, tx = rows_ref.shape[0], cols_ref.shape[0]
    sb = rows_ref.shape[1] // blocks
    fetches = [
        pltpu.make_async_copy(coil_any.at[:, half:, :], upper, sems.at[0]),
        pltpu.make_async_copy(coil_any.at[:, :half, :], coil.at[:, :half, :], sems.at[1]),
    ]
    for fetch in fetches:
        fetch.start()

    first = lax.broadcasted_iota(jnp.int32, (ty, half), 1) == 0
    for k in range(blocks):
        top = pl.multiple_of((tile_ref[k] // (ny // tx)) * ty, ty)
        here = slice(k * ty, (k + 1) * ty)
        for i in range(2):
            real = table_ref[pl.ds(i * ny + top, ty), :].astype(f32)
            imag = table_ref[pl.ds((2 + i) * ny + top, ty), :].astype(f32)
            odd = jnp.where(first, real[:, half:], -imag[:, :half])
            row = jnp.concatenate([real[:, :half], odd], axis=1).astype(bf16)
            for place in (0, 2) if i == 0 else (1,):
                fwd[here, place * ny : (place + 1) * ny] = row
    wide = blocks * ty
    for i in range(2):
        turned = fwd[:, i * ny : (i + 1) * ny].astype(f32).T.astype(bf16)
        for place in (0, 2) if i == 0 else (1,):
            adj[:, place * wide : (place + 1) * wide] = turned

    for k in range(blocks):
        left = pl.multiple_of(lax.rem(tile_ref[k], ny // tx) * tx, tx)
        chosen = [table_ref[pl.ds(i * ny + left, tx), :] for i in (0, 1, 2, 3)]
        stacked = jnp.concatenate(
            [jnp.concatenate([chosen[0], chosen[2]], axis=1), jnp.concatenate([chosen[1], chosen[3]], axis=1)], axis=0
        )
        here = slice(k * sb, (k + 1) * sb)
        cols = cols_ref[:, here]
        mixed = lax.dot_general(
            jnp.concatenate([cols, cols], axis=0), stacked, TN, preferred_element_type=f32
        )
        for ref, part in zip((whigh, wlow), split(mixed)):
            ref[k, :sb, :] = part[:, :ny]
            ref[k, sb:, :] = part[:, ny:]
        turned = rows_ref[:, here].astype(f32)
        row_weight = jnp.concatenate([turned, turned], axis=1)
        row_weight_ref[k] = row_weight
        cosine, sine = quarter_turn(cycle_ref[0], k)
        real, imag = data_ref[:, 0, here], data_ref[:, 1, here]
        values = jnp.concatenate([cosine * real + sine * imag, cosine * imag - sine * real], axis=1)
        spread(values, row_weight, whigh[k], wlow[k], xhigh, xlow, k, coils, ty)

    for fetch in fetches:
        fetch.wait()
    order = mirror(half)
    for c in range(coils):
        coil[c, half:, :] = matmul(order, upper[c]).astype(bf16)
    lower_rows, upper_rows = back_rows(adj, xhigh, xlow, coil, 0, coils)
    part_ref[:half, :] = lower_rows
    part_ref[half:ny, :] = upper_rows
    kept_ref[...] = weight_ref[...]
    count = weight_ref.shape[0]
    edge = jnp.concatenate([weight_ref[0:1, :], weight_ref[count - 1 : count, :]], axis=0)
    edge = jnp.concatenate([edge, jnp.zeros((6, edge.shape[1]), f32)], axis=0)
    part_ref[ny:, :] = jnp.concatenate([edge, jnp.zeros_like(edge)], axis=1)


def sum_kernel(ny, place_ref, *refs):
    parts, (folded_ref, image_ref, mine_ref) = refs[:-3], refs[-3:]
    total = parts[0][:ny, :]
    for part in parts[1:]:
        total = total + part[:ny, :]
    folded_ref[...] = total
    image_ref[: ny // 2, :] = total[: ny // 2]
    image_ref[ny // 2 :, :] = mirrored(total[ny // 2 :])
    count = mine_ref.shape[0]
    mine_ref[...] = image_ref[pl.ds(pl.multiple_of(place_ref[0] * count, count), count), :]


def predict_kernel(
    coils, blocks, cycle_ref, row_weight_ref, image_ref, fwd, coil, whigh, wlow, out_ref, thigh, tlow
):
    ny, nx = image_ref.shape[0], image_ref.shape[1] // 2
    half = ny // 2
    ty = row_weight_ref.shape[1]
    sb = row_weight_ref.shape[2] // 2
    edge = first_row(half, nx)
    for c in range(coils):
        products = []
        for i in range(2):
            here = slice(i * half, (i + 1) * half)
            coil_real = coil[c, here, :nx].astype(f32)
            coil_imag = coil[c, here, nx:].astype(f32)
            image_real, image_imag = image_ref[here, :nx], image_ref[here, nx:]
            products.append(coil_real * image_real - coil_imag * image_imag)
            products.append(coil_real * image_imag + coil_imag * image_real)
        lower_real, lower_imag, upper_real, upper_imag = products
        even = [
            lower_real + jnp.where(edge, 0.0, upper_real),
            lower_imag + jnp.where(edge, 0.0, upper_imag),
        ]
        odd = [
            jnp.where(edge, upper_real, lower_imag - upper_imag),
            jnp.where(edge, upper_imag, upper_real - lower_real),
        ]
        folded = jnp.concatenate([jnp.concatenate(even, axis=1), jnp.concatenate(odd, axis=1)], axis=0)
        high, low = split(folded)
        grid = matmul(fwd[...], jnp.concatenate([high, high, low], axis=0))
        for ref, part in zip((thigh, tlow), split(grid)):
            ref[:, 0, c * ty : (c + 1) * ty, :] = part[:, :nx].reshape(blocks, ty, nx)
            ref[:, 1, c * ty : (c + 1) * ty, :] = part[:, nx:].reshape(blocks, ty, nx)
    for k in range(blocks):
        left_high, left_low = (ref[k].reshape(2 * coils * ty, nx) for ref in (thigh, tlow))
        right_high = whigh[k]
        mixed = lax.dot_general(
            jnp.concatenate([left_high, left_low, left_high], axis=1),
            jnp.concatenate([right_high, right_high, wlow[k]], axis=1),
            NT,
            preferred_element_type=f32,
        )
        of_real, of_imag = mixed[: coils * ty], mixed[coils * ty :]
        product = jnp.concatenate(
            [of_real[:, :sb] - of_imag[:, sb:], of_real[:, sb:] + of_imag[:, :sb]], axis=1
        )
        summed = jnp.sum(product.reshape(coils, ty, 2 * sb) * row_weight_ref[k][None, :, :], axis=1)
        real, imag = summed[:, :sb], summed[:, sb:]
        cosine, sine = quarter_turn(cycle_ref[0], k)
        out_ref[k] = jnp.concatenate([cosine * real - sine * imag, sine * real + cosine * imag], axis=1)


def spread_kernel(coils, blocks, cycle_ref, row_weight_ref, whigh, wlow, *refs):
    parts, (xhigh, xlow, sums_ref) = refs[:-3], refs[-3:]
    ty = row_weight_ref.shape[1]
    sb = row_weight_ref.shape[2] // 2
    squares = 0.0
    for k in range(blocks):
        total = parts[0][k]
        for part in parts[1:]:
            total = total + part[k]
        squares += total * total
        cosine, sine = quarter_turn(cycle_ref[0], k)
        real, imag = total[:, :sb], total[:, sb:]
        values = jnp.concatenate([cosine * real + sine * imag, cosine * imag - sine * real], axis=1)
        spread(values, row_weight_ref[k], whigh[k], wlow[k], xhigh, xlow, k, coils, ty)
    lane = lax.broadcasted_iota(jnp.int32, sums_ref.shape, 1)
    sums_ref[...] = jnp.where(lane == 1, jnp.sum(squares), 0.0)


def rows_kernel(first, last, adj, coil, xhigh, xlow, *refs):
    out_ref = refs[-1]
    half = out_ref.shape[0] // 2
    for i, rows in enumerate(back_rows(adj, xhigh, xlow, coil, first, last)):
        here = slice(i * half, (i + 1) * half)
        out_ref[here, :] = rows + refs[0][here, :] if first else rows


def cut_kernel(place_ref, after_ref, folded_ref, *refs):
    *out_refs, whole = refs
    total = whole.shape[0]
    half = total // 2
    whole[:half, :] = folded_ref[:half, :]
    whole[half:, :] = mirrored(folded_ref[half:, :])
    for shift, out_ref in enumerate(out_refs):
        count = out_ref.shape[0]
        start = lax.rem(place_ref[0] + shift, total // count) * count
        out_ref[...] = whole[pl.ds(pl.multiple_of(start, count), count), :]


def neighbours(place_ref, image_ref, weight, before_ref, after_ref):
    count, nx = weight.shape
    total = image_ref.shape[0]
    place = place_ref[0]
    start = place * count
    weight_up = jnp.where(place > 0, before_ref[total + 1 : total + 2, :nx], 0.0)
    weight_down = jnp.where(place < total // count - 1, after_ref[total : total + 1, :nx], 0.0)
    image_up = image_ref[pl.ds(jnp.maximum(start - 1, 0), 1), :]
    image_down = image_ref[pl.ds(jnp.minimum(start + count, total - 1), 1), :]
    row = lax.broadcasted_iota(jnp.int32, (count, nx), 0)
    column = lax.broadcasted_iota(jnp.int32, (count, nx), 1)

    def above(values, edge):
        return jnp.where(row == 0, edge, pltpu.roll(values, 1, 0))

    def below(values, edge):
        return jnp.where(row == count - 1, edge, pltpu.roll(values, count - 1, 0))

    return weight_up, weight_down, image_up, image_down, column, above, below


def smooth_kernel(
    place_ref, image_ref, own_ref, even_ref, odd_ref, weight_ref, weight_even_ref, weight_odd_ref,
    before_ref, after_ref, out_ref, sums_ref,
):
    nx = image_ref.shape[1] // 2
    weight, weight_even, weight_odd = weight_ref[...], weight_even_ref[...], weight_odd_ref[...]
    weight_up, weight_down, image_up, image_down, column, above, below = neighbours(
        place_ref, image_ref, weight, before_ref, after_ref
    )
    weight_left = jnp.where(column == 0, 0.0, pltpu.roll(weight, 1, 1))
    weight_right = jnp.where(column == nx - 1, 0.0, pltpu.roll(weight, nx - 1, 1))
    weight_above, weight_below = above(weight, weight_up), below(weight, weight_down)
    squares = curvature = 0.0
    for part in range(2):
        lanes = slice(part * nx, (part + 1) * nx)
        here = own_ref[:, lanes]
        flux = weight_even * (here - even_ref[:, lanes]) + weight_odd * (here - odd_ref[:, lanes])
        flux += weight_above * (here - above(here, image_up[:, lanes]))
        flux += weight_below * (here - below(here, image_down[:, lanes]))
        flux += weight_left * (here - pltpu.roll(here, 1, 1))
        flux += weight_right * (here - pltpu.roll(here, nx - 1, 1))
        result = reg_strength * (weight * flux) + damping * here
        out_ref[:, lanes] = result
        squares += here * here
        curvature += here * result
    norm, energy = jnp.sum(squares), jnp.sum(curvature)
    lane = lax.broadcasted_iota(jnp.int32, sums_ref.shape, 1)
    sums_ref[...] = jnp.where(lane == 0, norm, jnp.where(lane == 1, energy, 0.0))


def update_kernel(images, own_ref, smooth_ref, *refs):
    image_refs, sums_refs, (field_ref, residual_ref) = refs[:images], refs[images:-2], refs[-2:]
    sums = sums_refs[0][0:1, :]
    for ref in sums_refs[1:]:
        sums = sums + ref[0:1, :]
    alpha = sums[:, 0:1] / sums[:, 1:2]
    here = own_ref[...]
    image = smooth_ref[...]
    for ref in image_refs:
        image = image + ref[...]
    field_ref[...] = alpha * here
    residual_ref[...] = here - alpha * image


def call(kernel, outs, specs, out_specs, scratch=(), flops=0, nbytes=0, limit=small_vmem):
    return pl.pallas_call(
        kernel,
        out_shape=outs,
        in_specs=specs,
        out_specs=out_specs,
        scratch_shapes=scratch,
        compiler_params=pltpu.CompilerParams(vmem_limit_bytes=limit),
        cost_estimate=pl.CostEstimate(flops=flops, bytes_accessed=nbytes, transcendentals=0),
    )


def shape(dims, dtype=f32):
    return jax.ShapeDtypeStruct(dims, dtype)


def exchange(values, axis, step):
    return lax.ppermute(values, axis, [(i, i ^ step) for i in range(lax.axis_size(axis))])


def powers(axis):
    return [1 << i for i in range(lax.axis_size(axis).bit_length() - 1)]


def from_others(values, axis):
    count = lax.axis_size(axis)
    return [
        lax.ppermute(values, axis, [(i, (i + shift) % count) for i in range(count)]) for shift in range(1, count)
    ]


def on_device(kspace_data, coil_maps, smooth_weight, kernel_cols, kernel_rows, tile_index, caipi_cycle):
    profiles, data, weight = coil_maps[0, 0], kspace_data[0], smooth_weight[0, 0]
    coils, ny, width = profiles.shape
    nx = width // 2
    blocks = tile_index.shape[0]
    samples, ty = kernel_rows.shape
    sb = samples // blocks
    count = weight.shape[0]
    rows, groups = lax.axis_size("row"), lax.axis_size("grp")
    row_place = lax.axis_index("row")
    table = jnp.asarray(dft_table(ny))
    wide = blocks * ty
    w_shape = (blocks, 2 * sb, nx)
    row_flops = 2 * 3 * coils * wide * ny * width
    col_flops = 2 * 3 * coils * ty * blocks * (2 * sb) * width
    place = jnp.stack([row_place, jnp.int32(rows)])
    dma = pltpu.SemaphoreType.DMA
    x_shape = pltpu.VMEM((coils, wide, width), bf16)

    data, weight, profiles, cols, rows_of, tile_index, table = (
        pltpu.with_memory_space_constraint(x, pltpu.HBM)
        for x in (data, weight, profiles, kernel_cols.T, kernel_rows.T, tile_index, table)
    )
    partial, *kept = call(
        functools.partial(rhs_kernel, coils, blocks),
        [
            shape((ny + 8, width)),
            pltpu.VMEM(w_shape, bf16),
            pltpu.VMEM(w_shape, bf16),
            pltpu.VMEM((wide, 3 * ny), bf16),
            pltpu.VMEM((ny, 3 * wide), bf16),
            pltpu.VMEM((blocks, ty, 2 * sb), f32),
            pltpu.VMEM(profiles.shape, bf16),
            pltpu.VMEM(weight.shape, f32),
        ],
        [SMEM, SMEM, SMEM, VMEM, VMEM, VMEM, VMEM, VMEM, HBM],
        [VMEM] * 8,
        [x_shape, x_shape, pltpu.VMEM((coils, ny // 2, width), bf16), dma((2,))],
        row_flops + 2 * col_flops,
        limit=large_vmem,
    )(place, tile_index, caipi_cycle, table, cols, rows_of, data, weight, profiles)
    whigh, wlow, fwd, adj, row_weight, coil, weight = (
        pltpu.with_memory_space_constraint(x, pltpu.VMEM) for x in kept
    )

    received = from_others(partial, "row")
    even_pairs = [(i, i ^ 1) for i in range(groups) if i ^ 1 < groups]
    odd_pairs = []
    for i in range(1, groups - 1, 2):
        odd_pairs += [(i, i + 1), (i + 1, i)]
    weights = [lax.ppermute(weight, "grp", pairs) for pairs in (even_pairs, odd_pairs)]
    folded, image, mine = call(
        functools.partial(sum_kernel, ny),
        [shape((ny, width)), shape((ny, width)), shape((count, width))],
        [SMEM] + [VMEM] * (1 + len(received)),
        [VMEM] * 3,
    )(place, partial, *received)
    others = [lax.ppermute(mine, "grp", pairs) for pairs in (even_pairs, odd_pairs)]

    predicted = call(
        functools.partial(predict_kernel, coils, blocks),
        shape((blocks, coils, 2 * sb)),
        [SMEM] + [VMEM] * 6,
        VMEM,
        [pltpu.VMEM((blocks, 2, coils * ty, nx), bf16)] * 2,
        row_flops + col_flops,
        limit=large_vmem,
    )(caipi_cycle, row_weight, folded, fwd, coil, whigh, wlow)

    predicted = [predicted, *from_others(predicted, "band")]
    smoothed, sums = call(
        smooth_kernel,
        [shape((count, width)), shape((8, 128))],
        [SMEM] + [VMEM] * 9,
        [VMEM, VMEM],
    )(place, image, mine, *others, weight, *weights, received[0], received[-1])
    for step in powers("band"):
        sums = sums + exchange(sums, "band", step)

    *kept, squares = call(
        functools.partial(spread_kernel, coils, blocks),
        [x_shape, x_shape, shape((8, 128))],
        [SMEM] + [VMEM] * (3 + len(predicted)),
        [VMEM] * 3,
        (),
        col_flops,
        limit=large_vmem,
    )(caipi_cycle, row_weight, whigh, wlow, *predicted)
    xhigh, xlow = (pltpu.with_memory_space_constraint(x, pltpu.VMEM) for x in kept)
    sums = sums + squares

    steps = powers("grp")
    for step in steps[:-1]:
        sums = sums + exchange(sums, "grp", step)
    middle = coils // 2

    def add_rows(first, last, *before):
        return call(
            functools.partial(rows_kernel, first, last),
            shape((ny, width)),
            [VMEM] * (4 + len(before)),
            VMEM,
            (),
            row_flops // 2,
            limit=large_vmem,
        )(adj, coil, xhigh, xlow, *before)

    unfinished = add_rows(middle, coils, add_rows(0, middle), sums)
    sums = sums + exchange(sums, "grp", steps[-1])
    halves = call(
        cut_kernel,
        [shape((count, width))] * 2 if rows == 2 else [shape((ny, width))],
        [SMEM] + [VMEM] * 2,
        [VMEM] * (2 if rows == 2 else 1),
        [pltpu.VMEM((ny, width), f32)],
    )(place, sums, unfinished)
    if rows == 2:
        images = [halves[0], exchange(halves[1], "row", 1)]
    else:
        images = [lax.psum_scatter(halves[0], "row", scatter_dimension=0, tiled=True)]
    all_sums = [sums, *from_others(sums, "row")]
    solution_field, residual = call(
        functools.partial(update_kernel, len(images)),
        [shape((count, width))] * 2,
        [VMEM] * (2 + len(images) + len(all_sums)),
        [VMEM, VMEM],
    )(mine, smoothed, *images, *all_sums)
    return solution_field[None, None], residual[None, None]


def solution(mesh):
    return jax.shard_map(
        on_device,
        mesh=mesh,
        in_specs=(
            P("grp", "row", None, None),
            P("band", "grp", "row", None, None),
            P("band", "grp", "row", None),
            P(),
            P(),
            P(),
            P("band"),
        ),
        out_specs=(P("band", "grp", "row", None), P("band", "grp", "row", None)),
        check_vma=False,
    )
```

```python
import functools
import math

import jax
import jax.numpy as jnp
import ml_dtypes
import numpy as np
from jax import lax
from jax.experimental import pallas as pl
from jax.experimental.pallas import tpu as pltpu
from jax.sharding import PartitionSpec as P

reg_strength = 0.5
damping = 1.0
f32 = jnp.float32
bf16 = jnp.bfloat16
VMEM = pl.BlockSpec(memory_space=pltpu.VMEM)
HBM = pl.BlockSpec(memory_space=pltpu.HBM)
TN = (((0,), (0,)), ((), ()))
NT = (((1,), (1,)), ((), ()))
large_vmem = 20 * 1024 * 1024
small_vmem = 8 * 1024 * 1024


def dft_table(length):
    index = np.arange(length)
    angle = (index[:, None] * index[None, :] % length) * (2.0 * np.pi / length)
    parts = []
    for part in (np.cos(angle) / math.sqrt(length), -np.sin(angle) / math.sqrt(length)):
        high = part.astype(ml_dtypes.bfloat16)
        low = (part - high.astype(np.float64)).astype(ml_dtypes.bfloat16)
        parts += [high, low]
    return np.concatenate(parts, axis=0)


def split(values):
    high = values.astype(bf16)
    return high, (values - high.astype(f32)).astype(bf16)


def matmul(left, right):
    return jnp.dot(left, right, preferred_element_type=f32)


def quarter_turn(cycle, block):
    turn = lax.rem(cycle * block, 4)
    one, zero = jnp.float32(1.0), jnp.float32(0.0)
    cosine = jnp.where(turn == 0, one, zero) - jnp.where(turn == 2, one, zero)
    sine = jnp.where(turn == 1, one, zero) - jnp.where(turn == 3, one, zero)
    return cosine, sine


def phase_of(phase_ref, block):
    return phase_ref[2 * block : 2 * block + 1, :], phase_ref[2 * block + 1 : 2 * block + 2, :]


def spread(values, row_weight, whigh, wlow, xhigh, xlow, k, coils, ty):
    weighted = values[:, None, :] * row_weight[None, :, :]
    parts = split(weighted.reshape(coils * ty, values.shape[1]))
    sb = values.shape[1] // 2
    vhigh, vlow = (
        jnp.concatenate([part, jnp.concatenate([part[:, sb:], -part[:, :sb]], axis=1)], axis=0) for part in parts
    )
    rows = matmul(
        jnp.concatenate([vhigh, vlow, vhigh], axis=1),
        jnp.concatenate([whigh, whigh, wlow], axis=0),
    )
    high, low = split(rows)
    there, nx = slice(k * ty, (k + 1) * ty), rows.shape[1]
    for part in range(2):
        for c in range(coils):
            here = slice((part * coils + c) * ty, (part * coils + c + 1) * ty)
            xhigh[c, there, part * nx : (part + 1) * nx] = high[here]
            xlow[c, there, part * nx : (part + 1) * nx] = low[here]


def mirror(rows):
    left = lax.broadcasted_iota(jnp.int32, (rows, rows), 0)
    right = lax.broadcasted_iota(jnp.int32, (rows, rows), 1)
    return (lax.rem(left + right, rows) == 0).astype(f32).astype(bf16)


def mirrored(values):
    high, rest = split(values)
    low = (values - high.astype(f32) - rest.astype(f32)).astype(bf16)
    order = mirror(values.shape[0])
    return matmul(order, high) + (matmul(order, rest) + matmul(order, low))


def first_row(rows, columns):
    return lax.broadcasted_iota(jnp.int32, (rows, columns), 0) == 0


def back_rows(adj, xhigh, xlow, coil, first, last):
    ny, nx = adj.shape[0], xhigh.shape[2] // 2
    half = ny // 2
    edge = first_row(half, nx)
    sums = [None] * 4
    for c in range(first, last):
        high, low = xhigh[c], xlow[c]
        folded = matmul(adj[...], jnp.concatenate([high, high, low], axis=0))
        even_real, even_imag = folded[:half, :nx], folded[:half, nx:]
        odd_real, odd_imag = folded[half:, :nx], folded[half:, nx:]
        lower = even_real - jnp.where(edge, 0.0, odd_imag), even_imag + jnp.where(edge, 0.0, odd_real)
        upper = jnp.where(edge, odd_real, even_real + odd_imag), jnp.where(edge, odd_imag, even_imag - odd_real)
        for i, (real, imag) in enumerate((lower, upper)):
            here = slice(i * half, (i + 1) * half)
            coil_real = coil[c, here, :nx].astype(f32)
            coil_imag = coil[c, here, nx:].astype(f32)
            terms = coil_real * real + coil_imag * imag, coil_real * imag - coil_imag * real
            for j, term in enumerate(terms):
                sums[2 * i + j] = term if c == first else sums[2 * i + j] + term
    return jnp.concatenate(sums[:2], axis=1), jnp.concatenate(sums[2:], axis=1)


def rhs_kernel(
    coils, blocks, cycle_ref, tile_any, table_any, cols_any, rows_any, data_any, weight_any, coil_any,
    part_ref, whigh, wlow, fwd, adj, row_weight_ref, coil, weight_ref, phase_ref,
    tile_ref, table_ref, cols_ref, rows_ref, data_ref, xhigh, xlow, upper, sems,
):
    ny = table_ref.shape[1]
    half = ny // 2
    ty, tx = rows_ref.shape[0], cols_ref.shape[0]
    sb = rows_ref.shape[1] // blocks
    moves = [
        (tile_any, tile_ref),
        (table_any, table_ref),
        (cols_any, cols_ref),
        (rows_any, rows_ref),
        (data_any, data_ref),
        (weight_any, weight_ref),
        (coil_any.at[:, half:, :], upper),
        (coil_any.at[:, :half, :], coil.at[:, :half, :]),
    ]
    fetches = [pltpu.make_async_copy(source, target, sems.at[i]) for i, (source, target) in enumerate(moves)]
    for fetch in fetches:
        fetch.start()
    for fetch in fetches[:-3]:
        fetch.wait()

    first = lax.broadcasted_iota(jnp.int32, (ty, half), 1) == 0
    for k in range(blocks):
        top = pl.multiple_of((tile_ref[k] // (ny // tx)) * ty, ty)
        here = slice(k * ty, (k + 1) * ty)
        for i in range(2):
            real = table_ref[pl.ds(i * ny + top, ty), :].astype(f32)
            imag = table_ref[pl.ds((2 + i) * ny + top, ty), :].astype(f32)
            odd = jnp.where(first, real[:, half:], -imag[:, :half])
            row = jnp.concatenate([real[:, :half], odd], axis=1).astype(bf16)
            for place in (0, 2) if i == 0 else (1,):
                fwd[here, place * ny : (place + 1) * ny] = row
    wide = blocks * ty
    for i in range(2):
        turned = fwd[:, i * ny : (i + 1) * ny].astype(f32).T.astype(bf16)
        for place in (0, 2) if i == 0 else (1,):
            adj[:, place * wide : (place + 1) * wide] = turned

    for k in range(blocks):
        left = pl.multiple_of(lax.rem(tile_ref[k], ny // tx) * tx, tx)
        chosen = [table_ref[pl.ds(i * ny + left, tx), :] for i in (0, 1, 2, 3)]
        stacked = jnp.concatenate(
            [jnp.concatenate([chosen[0], chosen[2]], axis=1), jnp.concatenate([chosen[1], chosen[3]], axis=1)], axis=0
        )
        here = slice(k * sb, (k + 1) * sb)
        cols = cols_ref[:, here]
        mixed = lax.dot_general(
            jnp.concatenate([cols, cols], axis=0), stacked, TN, preferred_element_type=f32
        )
        for ref, part in zip((whigh, wlow), split(mixed)):
            ref[k, :sb, :] = part[:, :ny]
            ref[k, sb:, :] = part[:, ny:]
        turned = rows_ref[:, here].astype(f32)
        row_weight = jnp.concatenate([turned, turned], axis=1)
        row_weight_ref[k] = row_weight
        for i, part in enumerate(quarter_turn(cycle_ref[0], k)):
            phase_ref[2 * k + i : 2 * k + i + 1, :] = jnp.full((1, sb), part, f32)
        cosine, sine = phase_of(phase_ref, k)
        real, imag = data_ref[:, 0, here], data_ref[:, 1, here]
        values = jnp.concatenate([cosine * real + sine * imag, cosine * imag - sine * real], axis=1)
        spread(values, row_weight, whigh[k], wlow[k], xhigh, xlow, k, coils, ty)

    for fetch in fetches[-3:]:
        fetch.wait()
    order = mirror(half)
    for c in range(coils):
        coil[c, half:, :] = matmul(order, upper[c]).astype(bf16)
    lower_rows, upper_rows = back_rows(adj, xhigh, xlow, coil, 0, coils)
    part_ref[:half, :] = lower_rows
    part_ref[half:ny, :] = upper_rows
    count = weight_ref.shape[0]
    edge = jnp.concatenate([weight_ref[0:1, :], weight_ref[count - 1 : count, :]], axis=0)
    edge = jnp.concatenate([edge, jnp.zeros((6, edge.shape[1]), f32)], axis=0)
    part_ref[ny:, :] = jnp.concatenate([edge, jnp.zeros_like(edge)], axis=1)


def sum_kernel(ny, *refs):
    parts, (folded_ref, image_ref, mine_ref) = refs[:-3], refs[-3:]
    total = parts[0][:ny, :]
    for part in parts[1:]:
        total = total + part[:ny, :]
    folded_ref[...] = total
    image_ref[: ny // 2, :] = total[: ny // 2]
    image_ref[ny // 2 :, :] = mirrored(total[ny // 2 :])
    count = mine_ref.shape[0]
    mine_ref[...] = image_ref[pl.ds(pl.multiple_of(lax.axis_index("row") * count, count), count), :]


def predict_kernel(
    coils, blocks, phase_ref, row_weight_ref, image_ref, fwd, coil, whigh, wlow, out_ref, thigh, tlow
):
    ny, nx = image_ref.shape[0], image_ref.shape[1] // 2
    half = ny // 2
    ty = row_weight_ref.shape[1]
    sb = row_weight_ref.shape[2] // 2
    edge = first_row(half, nx)
    for c in range(coils):
        products = []
        for i in range(2):
            here = slice(i * half, (i + 1) * half)
            coil_real = coil[c, here, :nx].astype(f32)
            coil_imag = coil[c, here, nx:].astype(f32)
            image_real, image_imag = image_ref[here, :nx], image_ref[here, nx:]
            products.append(coil_real * image_real - coil_imag * image_imag)
            products.append(coil_real * image_imag + coil_imag * image_real)
        lower_real, lower_imag, upper_real, upper_imag = products
        even = [
            lower_real + jnp.where(edge, 0.0, upper_real),
            lower_imag + jnp.where(edge, 0.0, upper_imag),
        ]
        odd = [
            jnp.where(edge, upper_real, lower_imag - upper_imag),
            jnp.where(edge, upper_imag, upper_real - lower_real),
        ]
        folded = jnp.concatenate([jnp.concatenate(even, axis=1), jnp.concatenate(odd, axis=1)], axis=0)
        high, low = split(folded)
        grid = matmul(fwd[...], jnp.concatenate([high, high, low], axis=0))
        for ref, part in zip((thigh, tlow), split(grid)):
            ref[:, 0, c * ty : (c + 1) * ty, :] = part[:, :nx].reshape(blocks, ty, nx)
            ref[:, 1, c * ty : (c + 1) * ty, :] = part[:, nx:].reshape(blocks, ty, nx)
    for k in range(blocks):
        left_high, left_low = (ref[k].reshape(2 * coils * ty, nx) for ref in (thigh, tlow))
        right_high = whigh[k]
        mixed = lax.dot_general(
            jnp.concatenate([left_high, left_low, left_high], axis=1),
            jnp.concatenate([right_high, right_high, wlow[k]], axis=1),
            NT,
            preferred_element_type=f32,
        )
        of_real, of_imag = mixed[: coils * ty], mixed[coils * ty :]
        product = jnp.concatenate(
            [of_real[:, :sb] - of_imag[:, sb:], of_real[:, sb:] + of_imag[:, :sb]], axis=1
        )
        summed = jnp.sum(product.reshape(coils, ty, 2 * sb) * row_weight_ref[k][None, :, :], axis=1)
        real, imag = summed[:, :sb], summed[:, sb:]
        cosine, sine = phase_of(phase_ref, k)
        out_ref[k] = jnp.concatenate([cosine * real - sine * imag, sine * real + cosine * imag], axis=1)


def spread_kernel(coils, blocks, phase_ref, row_weight_ref, whigh, wlow, *refs):
    parts, (xhigh, xlow, sums_ref) = refs[:-3], refs[-3:]
    ty = row_weight_ref.shape[1]
    sb = row_weight_ref.shape[2] // 2
    squares = 0.0
    for k in range(blocks):
        total = parts[0][k]
        for part in parts[1:]:
            total = total + part[k]
        squares += total * total
        cosine, sine = phase_of(phase_ref, k)
        real, imag = total[:, :sb], total[:, sb:]
        values = jnp.concatenate([cosine * real + sine * imag, cosine * imag - sine * real], axis=1)
        spread(values, row_weight_ref[k], whigh[k], wlow[k], xhigh, xlow, k, coils, ty)
    lane = lax.broadcasted_iota(jnp.int32, sums_ref.shape, 1)
    sums_ref[...] = jnp.where(lane == 1, jnp.sum(squares), 0.0)


def rows_kernel(first, last, adj, coil, xhigh, xlow, *refs):
    out_ref = refs[-1]
    half = out_ref.shape[0] // 2
    for i, rows in enumerate(back_rows(adj, xhigh, xlow, coil, first, last)):
        here = slice(i * half, (i + 1) * half)
        out_ref[here, :] = rows + refs[0][here, :] if first else rows


def cut_kernel(after_ref, folded_ref, *refs):
    *out_refs, whole = refs
    total = whole.shape[0]
    half = total // 2
    whole[:half, :] = folded_ref[:half, :]
    whole[half:, :] = mirrored(folded_ref[half:, :])
    for shift, out_ref in enumerate(out_refs):
        count = out_ref.shape[0]
        start = lax.rem(lax.axis_index("row") + shift, total // count) * count
        out_ref[...] = whole[pl.ds(pl.multiple_of(start, count), count), :]


def neighbours(image_ref, weight, before_ref, after_ref):
    count, nx = weight.shape
    total = image_ref.shape[0]
    place = lax.axis_index("row")
    start = place * count
    weight_up = jnp.where(place > 0, before_ref[total + 1 : total + 2, :nx], 0.0)
    weight_down = jnp.where(place < total // count - 1, after_ref[total : total + 1, :nx], 0.0)
    image_up = image_ref[pl.ds(jnp.maximum(start - 1, 0), 1), :]
    image_down = image_ref[pl.ds(jnp.minimum(start + count, total - 1), 1), :]
    row = lax.broadcasted_iota(jnp.int32, (count, nx), 0)
    column = lax.broadcasted_iota(jnp.int32, (count, nx), 1)

    def above(values, edge):
        return jnp.where(row == 0, edge, pltpu.roll(values, 1, 0))

    def below(values, edge):
        return jnp.where(row == count - 1, edge, pltpu.roll(values, count - 1, 0))

    return weight_up, weight_down, image_up, image_down, column, above, below


def smooth_kernel(
    image_ref, own_ref, even_ref, odd_ref, weight_ref, weight_even_ref, weight_odd_ref,
    before_ref, after_ref, out_ref, sums_ref,
):
    nx = image_ref.shape[1] // 2
    weight, weight_even, weight_odd = weight_ref[...], weight_even_ref[...], weight_odd_ref[...]
    weight_up, weight_down, image_up, image_down, column, above, below = neighbours(
        image_ref, weight, before_ref, after_ref
    )
    weight_left = jnp.where(column == 0, 0.0, pltpu.roll(weight, 1, 1))
    weight_right = jnp.where(column == nx - 1, 0.0, pltpu.roll(weight, nx - 1, 1))
    weight_above, weight_below = above(weight, weight_up), below(weight, weight_down)
    squares = curvature = 0.0
    for part in range(2):
        lanes = slice(part * nx, (part + 1) * nx)
        here = own_ref[:, lanes]
        flux = weight_even * (here - even_ref[:, lanes]) + weight_odd * (here - odd_ref[:, lanes])
        flux += weight_above * (here - above(here, image_up[:, lanes]))
        flux += weight_below * (here - below(here, image_down[:, lanes]))
        flux += weight_left * (here - pltpu.roll(here, 1, 1))
        flux += weight_right * (here - pltpu.roll(here, nx - 1, 1))
        result = reg_strength * (weight * flux) + damping * here
        out_ref[:, lanes] = result
        squares += here * here
        curvature += here * result
    norm, energy = jnp.sum(squares), jnp.sum(curvature)
    lane = lax.broadcasted_iota(jnp.int32, sums_ref.shape, 1)
    sums_ref[...] = jnp.where(lane == 0, norm, jnp.where(lane == 1, energy, 0.0))


def update_kernel(images, own_ref, smooth_ref, *refs):
    image_refs, sums_refs, (field_ref, residual_ref) = refs[:images], refs[images:-2], refs[-2:]
    sums = sums_refs[0][0:1, :]
    for ref in sums_refs[1:]:
        sums = sums + ref[0:1, :]
    alpha = sums[:, 0:1] / sums[:, 1:2]
    here = own_ref[...]
    image = smooth_ref[...]
    for ref in image_refs:
        image = image + ref[...]
    field_ref[...] = alpha * here
    residual_ref[...] = here - alpha * image


def call(kernel, outs, specs, out_specs, scratch=(), flops=0, nbytes=0, limit=small_vmem):
    return pl.pallas_call(
        kernel,
        out_shape=outs,
        in_specs=specs,
        out_specs=out_specs,
        scratch_shapes=scratch,
        compiler_params=pltpu.CompilerParams(vmem_limit_bytes=limit),
        cost_estimate=pl.CostEstimate(flops=flops, bytes_accessed=nbytes, transcendentals=0),
    )


def shape(dims, dtype=f32):
    return jax.ShapeDtypeStruct(dims, dtype)


def exchange(values, axis, step):
    return lax.ppermute(values, axis, [(i, i ^ step) for i in range(lax.axis_size(axis))])


def powers(axis):
    return [1 << i for i in range(lax.axis_size(axis).bit_length() - 1)]


def from_others(values, axis):
    count = lax.axis_size(axis)
    return [
        lax.ppermute(values, axis, [(i, (i + shift) % count) for i in range(count)]) for shift in range(1, count)
    ]


def on_device(kspace_data, coil_maps, smooth_weight, kernel_cols, kernel_rows, tile_index, caipi_cycle):
    profiles, data, weight = coil_maps[0, 0], kspace_data[0], smooth_weight[0, 0]
    coils, ny, width = profiles.shape
    nx = width // 2
    blocks = tile_index.shape[0]
    samples, ty = kernel_rows.shape
    sb = samples // blocks
    count = weight.shape[0]
    rows, groups = lax.axis_size("row"), lax.axis_size("grp")
    table = jnp.asarray(dft_table(ny))
    wide = blocks * ty
    w_shape = (blocks, 2 * sb, nx)
    row_flops = 2 * 3 * coils * wide * ny * width
    col_flops = 2 * 3 * coils * ty * blocks * (2 * sb) * width
    dma = pltpu.SemaphoreType.DMA
    x_shape = pltpu.VMEM((coils, wide, width), bf16)

    inputs = [tile_index, table, kernel_cols.T, kernel_rows.T, data, weight, profiles]
    fetched = [
        pltpu.SMEM(tile_index.shape, tile_index.dtype),
        *[pltpu.VMEM(x.shape, x.dtype) for x in inputs[1:5]],
    ]
    partial, *kept = call(
        functools.partial(rhs_kernel, coils, blocks),
        [
            shape((ny + 8, width)),
            pltpu.VMEM(w_shape, bf16),
            pltpu.VMEM(w_shape, bf16),
            pltpu.VMEM((wide, 3 * ny), bf16),
            pltpu.VMEM((ny, 3 * wide), bf16),
            pltpu.VMEM((blocks, ty, 2 * sb), f32),
            pltpu.VMEM(profiles.shape, bf16),
            pltpu.VMEM(weight.shape, f32),
            pltpu.VMEM((2 * blocks, sb), f32),
        ],
        [pl.BlockSpec(memory_space=pltpu.SMEM)] + [HBM] * len(inputs),
        [VMEM] * 9,
        [*fetched, x_shape, x_shape, pltpu.VMEM((coils, ny // 2, width), bf16), dma((len(inputs) + 1,))],
        row_flops + 2 * col_flops,
        limit=large_vmem,
    )(caipi_cycle, *(pltpu.with_memory_space_constraint(x, pltpu.HBM) for x in inputs))
    whigh, wlow, fwd, adj, row_weight, coil, weight, phases = (
        pltpu.with_memory_space_constraint(x, pltpu.VMEM) for x in kept
    )

    received = from_others(partial, "row")
    even_pairs = [(i, i ^ 1) for i in range(groups) if i ^ 1 < groups]
    odd_pairs = []
    for i in range(1, groups - 1, 2):
        odd_pairs += [(i, i + 1), (i + 1, i)]
    weights = [lax.ppermute(weight, "grp", pairs) for pairs in (even_pairs, odd_pairs)]
    folded, image, mine = call(
        functools.partial(sum_kernel, ny),
        [shape((ny, width)), shape((ny, width)), shape((count, width))],
        [VMEM] * (1 + len(received)),
        [VMEM] * 3,
    )(partial, *received)
    others = [lax.ppermute(mine, "grp", pairs) for pairs in (even_pairs, odd_pairs)]

    predicted = call(
        functools.partial(predict_kernel, coils, blocks),
        shape((blocks, coils, 2 * sb)),
        [VMEM] * 7,
        VMEM,
        [pltpu.VMEM((blocks, 2, coils * ty, nx), bf16)] * 2,
        row_flops + col_flops,
        limit=large_vmem,
    )(phases, row_weight, folded, fwd, coil, whigh, wlow)

    predicted = [predicted, *[exchange(predicted, "band", step) for step in range(lax.axis_size("band") - 1, 0, -1)]]
    smoothed, sums = call(
        smooth_kernel,
        [shape((count, width)), shape((8, 128))],
        [VMEM] * 9,
        [VMEM, VMEM],
    )(image, mine, *others, weight, *weights, received[0], received[-1])
    bands = range(lax.axis_size("band") - 1, 0, -1)
    sums = [sums, *[exchange(sums, "band", step) for step in bands]]

    *kept, squares = call(
        functools.partial(spread_kernel, coils, blocks),
        [x_shape, x_shape, shape((8, 128))],
        [VMEM] * (4 + len(predicted)),
        [VMEM] * 3,
        (),
        col_flops,
        limit=large_vmem,
    )(phases, row_weight, whigh, wlow, *predicted)
    xhigh, xlow = (pltpu.with_memory_space_constraint(x, pltpu.VMEM) for x in kept)
    sums = sum(sums) + squares

    steps = powers("grp")
    for step in steps[:-1]:
        sums = sums + exchange(sums, "grp", step)
    middle = coils // 2

    def add_rows(first, last, *before):
        return call(
            functools.partial(rows_kernel, first, last),
            shape((ny, width)),
            [VMEM] * (4 + len(before)),
            VMEM,
            (),
            row_flops // 2,
            limit=large_vmem,
        )(adj, coil, xhigh, xlow, *before)

    unfinished = add_rows(middle, coils, add_rows(0, middle), sums)
    sums = sums + exchange(sums, "grp", steps[-1])
    halves = call(
        cut_kernel,
        [shape((count, width))] * 2 if rows == 2 else [shape((ny, width))],
        [VMEM] * 2,
        [VMEM] * (2 if rows == 2 else 1),
        [pltpu.VMEM((ny, width), f32)],
    )(sums, unfinished)
    if rows == 2:
        images = [halves[0], exchange(halves[1], "row", 1)]
    else:
        images = [lax.psum_scatter(halves[0], "row", scatter_dimension=0, tiled=True)]
    all_sums = [sums, *from_others(sums, "row")]
    solution_field, residual = call(
        functools.partial(update_kernel, len(images)),
        [shape((count, width))] * 2,
        [VMEM] * (2 + len(images) + len(all_sums)),
        [VMEM, VMEM],
    )(mine, smoothed, *images, *all_sums)
    return solution_field[None, None], residual[None, None]


def solution(mesh):
    return jax.shard_map(
        on_device,
        mesh=mesh,
        in_specs=(
            P("grp", "row", None, None),
            P("band", "grp", "row", None, None),
            P("band", "grp", "row", None),
            P(),
            P(),
            P(),
            P("band"),
        ),
        out_specs=(P("band", "grp", "row", None), P("band", "grp", "row", None)),
        check_vma=False,
    )
```

```python
import functools
import math

import jax
import jax.numpy as jnp
import ml_dtypes
import numpy as np
from jax import lax
from jax.experimental import pallas as pl
from jax.experimental.pallas import tpu as pltpu
from jax.sharding import PartitionSpec as P

reg_strength = 0.5
damping = 1.0
f32 = jnp.float32
bf16 = jnp.bfloat16
VMEM = pl.BlockSpec(memory_space=pltpu.VMEM)
HBM = pl.BlockSpec(memory_space=pltpu.HBM)
TN = (((0,), (0,)), ((), ()))
NT = (((1,), (1,)), ((), ()))
large_vmem = 20 * 1024 * 1024
small_vmem = 8 * 1024 * 1024


def dft_table(length):
    index = np.arange(length)
    angle = (index[:, None] * index[None, :] % length) * (2.0 * np.pi / length)
    parts = []
    for part in (np.cos(angle) / math.sqrt(length), -np.sin(angle) / math.sqrt(length)):
        high = part.astype(ml_dtypes.bfloat16)
        low = (part - high.astype(np.float64)).astype(ml_dtypes.bfloat16)
        parts += [high, low]
    return np.concatenate(parts, axis=0)


def split(values):
    high = values.astype(bf16)
    return high, (values - high.astype(f32)).astype(bf16)


def matmul(left, right):
    return jnp.dot(left, right, preferred_element_type=f32)


def quarter_turn(cycle, block):
    turn = lax.rem(cycle * block, 4)
    one, zero = jnp.float32(1.0), jnp.float32(0.0)
    cosine = jnp.where(turn == 0, one, zero) - jnp.where(turn == 2, one, zero)
    sine = jnp.where(turn == 1, one, zero) - jnp.where(turn == 3, one, zero)
    return cosine, sine


def phase_of(phase_ref, block):
    return phase_ref[2 * block : 2 * block + 1, :], phase_ref[2 * block + 1 : 2 * block + 2, :]


def spread(values, row_weight, whigh, wlow, xhigh, xlow, k, coils, ty):
    weighted = values[:, None, :] * row_weight[None, :, :]
    parts = split(weighted.reshape(coils * ty, values.shape[1]))
    sb = values.shape[1] // 2
    vhigh, vlow = (
        jnp.concatenate([part, jnp.concatenate([part[:, sb:], -part[:, :sb]], axis=1)], axis=0) for part in parts
    )
    rows = matmul(
        jnp.concatenate([vhigh, vlow, vhigh], axis=1),
        jnp.concatenate([whigh, whigh, wlow], axis=0),
    )
    high, low = split(rows)
    there, nx = slice(k * ty, (k + 1) * ty), rows.shape[1]
    for part in range(2):
        for c in range(coils):
            here = slice((part * coils + c) * ty, (part * coils + c + 1) * ty)
            xhigh[c, there, part * nx : (part + 1) * nx] = high[here]
            xlow[c, there, part * nx : (part + 1) * nx] = low[here]


def mirror(rows):
    left = lax.broadcasted_iota(jnp.int32, (rows, rows), 0)
    right = lax.broadcasted_iota(jnp.int32, (rows, rows), 1)
    return (lax.rem(left + right, rows) == 0).astype(f32).astype(bf16)


def mirrored(values):
    high, rest = split(values)
    low = (values - high.astype(f32) - rest.astype(f32)).astype(bf16)
    order = mirror(values.shape[0])
    return matmul(order, high) + (matmul(order, rest) + matmul(order, low))


def first_row(rows, columns):
    return lax.broadcasted_iota(jnp.int32, (rows, columns), 0) == 0


def back_rows(adj, xhigh, xlow, coil, first, last):
    ny, nx = adj.shape[0], xhigh.shape[2] // 2
    half = ny // 2
    edge = first_row(half, nx)
    sums = [None] * 4
    for c in range(first, last):
        high, low = xhigh[c], xlow[c]
        folded = matmul(adj[...], jnp.concatenate([high, high, low], axis=0))
        even_real, even_imag = folded[:half, :nx], folded[:half, nx:]
        odd_real, odd_imag = folded[half:, :nx], folded[half:, nx:]
        lower = even_real - jnp.where(edge, 0.0, odd_imag), even_imag + jnp.where(edge, 0.0, odd_real)
        upper = jnp.where(edge, odd_real, even_real + odd_imag), jnp.where(edge, odd_imag, even_imag - odd_real)
        for i, (real, imag) in enumerate((lower, upper)):
            here = slice(i * half, (i + 1) * half)
            coil_real = coil[c, here, :nx].astype(f32)
            coil_imag = coil[c, here, nx:].astype(f32)
            terms = coil_real * real + coil_imag * imag, coil_real * imag - coil_imag * real
            for j, term in enumerate(terms):
                sums[2 * i + j] = term if c == first else sums[2 * i + j] + term
    return jnp.concatenate(sums[:2], axis=1), jnp.concatenate(sums[2:], axis=1)


def tables_kernel(
    coils, blocks, cycle_ref, tile_any, table_any, cols_any, rows_any, data_any, weight_any, coil_any,
    whigh, wlow, fwd, adj, row_weight_ref, coil, weight_ref, phase_ref, data_ref,
    tile_ref, table_ref, cols_ref, rows_ref, upper, sems,
):
    ny = table_ref.shape[1]
    half = ny // 2
    ty, tx = rows_ref.shape[0], cols_ref.shape[0]
    sb = rows_ref.shape[1] // blocks
    moves = [
        (tile_any, tile_ref),
        (table_any, table_ref),
        (cols_any, cols_ref),
        (rows_any, rows_ref),
        (data_any, data_ref),
        (weight_any, weight_ref),
        (coil_any.at[:, half:, :], upper),
        (coil_any.at[:, :half, :], coil.at[:, :half, :]),
    ]
    fetches = [pltpu.make_async_copy(source, target, sems.at[i]) for i, (source, target) in enumerate(moves)]
    for fetch in fetches:
        fetch.start()
    for fetch in fetches[:-3]:
        fetch.wait()

    first = lax.broadcasted_iota(jnp.int32, (ty, half), 1) == 0
    for k in range(blocks):
        top = pl.multiple_of((tile_ref[k] // (ny // tx)) * ty, ty)
        here = slice(k * ty, (k + 1) * ty)
        for i in range(2):
            real = table_ref[pl.ds(i * ny + top, ty), :].astype(f32)
            imag = table_ref[pl.ds((2 + i) * ny + top, ty), :].astype(f32)
            odd = jnp.where(first, real[:, half:], -imag[:, :half])
            row = jnp.concatenate([real[:, :half], odd], axis=1).astype(bf16)
            for place in (0, 2) if i == 0 else (1,):
                fwd[here, place * ny : (place + 1) * ny] = row
    wide = blocks * ty
    for i in range(2):
        turned = fwd[:, i * ny : (i + 1) * ny].astype(f32).T.astype(bf16)
        for place in (0, 2) if i == 0 else (1,):
            adj[:, place * wide : (place + 1) * wide] = turned

    for k in range(blocks):
        left = pl.multiple_of(lax.rem(tile_ref[k], ny // tx) * tx, tx)
        chosen = [table_ref[pl.ds(i * ny + left, tx), :] for i in (0, 1, 2, 3)]
        stacked = jnp.concatenate(
            [jnp.concatenate([chosen[0], chosen[2]], axis=1), jnp.concatenate([chosen[1], chosen[3]], axis=1)], axis=0
        )
        here = slice(k * sb, (k + 1) * sb)
        cols = cols_ref[:, here]
        mixed = lax.dot_general(
            jnp.concatenate([cols, cols], axis=0), stacked, TN, preferred_element_type=f32
        )
        for ref, part in zip((whigh, wlow), split(mixed)):
            ref[k, :sb, :] = part[:, :ny]
            ref[k, sb:, :] = part[:, ny:]
        turned = rows_ref[:, here].astype(f32)
        row_weight = jnp.concatenate([turned, turned], axis=1)
        row_weight_ref[k] = row_weight
        for i, part in enumerate(quarter_turn(cycle_ref[0], k)):
            phase_ref[2 * k + i : 2 * k + i + 1, :] = jnp.full((1, sb), part, f32)
    for fetch in fetches[-3:]:
        fetch.wait()
    order = mirror(half)
    for c in range(coils):
        coil[c, half:, :] = matmul(order, upper[c]).astype(bf16)


def rhs_kernel(
    coils, blocks, phase_ref, row_weight_ref, whigh, wlow, adj, coil, data_ref, weight_ref, part_ref, xhigh, xlow
):
    ny = adj.shape[0]
    half = ny // 2
    ty = row_weight_ref.shape[1]
    sb = row_weight_ref.shape[2] // 2
    for k in range(blocks):
        here = slice(k * sb, (k + 1) * sb)
        cosine, sine = phase_of(phase_ref, k)
        real, imag = data_ref[:, 0, here], data_ref[:, 1, here]
        values = jnp.concatenate([cosine * real + sine * imag, cosine * imag - sine * real], axis=1)
        spread(values, row_weight_ref[k], whigh[k], wlow[k], xhigh, xlow, k, coils, ty)
    lower_rows, upper_rows = back_rows(adj, xhigh, xlow, coil, 0, coils)
    part_ref[:half, :] = lower_rows
    part_ref[half:ny, :] = upper_rows
    count = weight_ref.shape[0]
    edge = jnp.concatenate([weight_ref[0:1, :], weight_ref[count - 1 : count, :]], axis=0)
    edge = jnp.concatenate([edge, jnp.zeros((6, edge.shape[1]), f32)], axis=0)
    part_ref[ny:, :] = jnp.concatenate([edge, jnp.zeros_like(edge)], axis=1)


def sum_kernel(ny, *refs):
    parts, (folded_ref, image_ref, mine_ref) = refs[:-3], refs[-3:]
    total = parts[0][:ny, :]
    for part in parts[1:]:
        total = total + part[:ny, :]
    folded_ref[...] = total
    image_ref[: ny // 2, :] = total[: ny // 2]
    image_ref[ny // 2 :, :] = mirrored(total[ny // 2 :])
    count = mine_ref.shape[0]
    mine_ref[...] = image_ref[pl.ds(pl.multiple_of(lax.axis_index("row") * count, count), count), :]


def predict_kernel(
    coils, blocks, phase_ref, row_weight_ref, image_ref, fwd, coil, whigh, wlow, out_ref, thigh, tlow
):
    ny, nx = image_ref.shape[0], image_ref.shape[1] // 2
    half = ny // 2
    ty = row_weight_ref.shape[1]
    sb = row_weight_ref.shape[2] // 2
    edge = first_row(half, nx)
    for c in range(coils):
        products = []
        for i in range(2):
            here = slice(i * half, (i + 1) * half)
            coil_real = coil[c, here, :nx].astype(f32)
            coil_imag = coil[c, here, nx:].astype(f32)
            image_real, image_imag = image_ref[here, :nx], image_ref[here, nx:]
            products.append(coil_real * image_real - coil_imag * image_imag)
            products.append(coil_real * image_imag + coil_imag * image_real)
        lower_real, lower_imag, upper_real, upper_imag = products
        even = [
            lower_real + jnp.where(edge, 0.0, upper_real),
            lower_imag + jnp.where(edge, 0.0, upper_imag),
        ]
        odd = [
            jnp.where(edge, upper_real, lower_imag - upper_imag),
            jnp.where(edge, upper_imag, upper_real - lower_real),
        ]
        folded = jnp.concatenate([jnp.concatenate(even, axis=1), jnp.concatenate(odd, axis=1)], axis=0)
        high, low = split(folded)
        grid = matmul(fwd[...], jnp.concatenate([high, high, low], axis=0))
        for ref, part in zip((thigh, tlow), split(grid)):
            ref[:, 0, c * ty : (c + 1) * ty, :] = part[:, :nx].reshape(blocks, ty, nx)
            ref[:, 1, c * ty : (c + 1) * ty, :] = part[:, nx:].reshape(blocks, ty, nx)
    for k in range(blocks):
        left_high, left_low = (ref[k].reshape(2 * coils * ty, nx) for ref in (thigh, tlow))
        right_high = whigh[k]
        mixed = lax.dot_general(
            jnp.concatenate([left_high, left_low, left_high], axis=1),
            jnp.concatenate([right_high, right_high, wlow[k]], axis=1),
            NT,
            preferred_element_type=f32,
        )
        of_real, of_imag = mixed[: coils * ty], mixed[coils * ty :]
        product = jnp.concatenate(
            [of_real[:, :sb] - of_imag[:, sb:], of_real[:, sb:] + of_imag[:, :sb]], axis=1
        )
        summed = jnp.sum(product.reshape(coils, ty, 2 * sb) * row_weight_ref[k][None, :, :], axis=1)
        real, imag = summed[:, :sb], summed[:, sb:]
        cosine, sine = phase_of(phase_ref, k)
        out_ref[k] = jnp.concatenate([cosine * real - sine * imag, sine * real + cosine * imag], axis=1)


def collapse_kernel(bands, *refs):
    parts, sums_refs, (out_ref, out_sums_ref) = refs[:bands], refs[bands:-2], refs[-2:]
    total = parts[0][...]
    for part in parts[1:]:
        total = total + part[...]
    out_ref[...] = total
    sums = sums_refs[0][...]
    for ref in sums_refs[1:]:
        sums = sums + ref[...]
    lane = lax.broadcasted_iota(jnp.int32, sums.shape, 1)
    squares = jnp.sum(jnp.sum(total * total, axis=0))
    out_sums_ref[...] = jnp.where(lane == 1, sums + squares, sums)


def spread_kernel(coils, blocks, phase_ref, row_weight_ref, whigh, wlow, collapsed_ref, xhigh, xlow):
    ty = row_weight_ref.shape[1]
    sb = row_weight_ref.shape[2] // 2
    for k in range(blocks):
        cosine, sine = phase_of(phase_ref, k)
        real, imag = collapsed_ref[k, :, :sb], collapsed_ref[k, :, sb:]
        values = jnp.concatenate([cosine * real + sine * imag, cosine * imag - sine * real], axis=1)
        spread(values, row_weight_ref[k], whigh[k], wlow[k], xhigh, xlow, k, coils, ty)


def rows_kernel(first, last, adj, coil, xhigh, xlow, *refs):
    out_ref = refs[-1]
    half = out_ref.shape[0] // 2
    for i, rows in enumerate(back_rows(adj, xhigh, xlow, coil, first, last)):
        here = slice(i * half, (i + 1) * half)
        out_ref[here, :] = rows + refs[0][here, :] if first else rows


def cut_kernel(after_ref, folded_ref, *refs):
    *out_refs, whole = refs
    total = whole.shape[0]
    half = total // 2
    whole[:half, :] = folded_ref[:half, :]
    whole[half:, :] = mirrored(folded_ref[half:, :])
    for shift, out_ref in enumerate(out_refs):
        count = out_ref.shape[0]
        start = lax.rem(lax.axis_index("row") + shift, total // count) * count
        out_ref[...] = whole[pl.ds(pl.multiple_of(start, count), count), :]


def neighbours(image_ref, weight, before_ref, after_ref):
    count, nx = weight.shape
    total = image_ref.shape[0]
    place = lax.axis_index("row")
    start = place * count
    weight_up = jnp.where(place > 0, before_ref[total + 1 : total + 2, :nx], 0.0)
    weight_down = jnp.where(place < total // count - 1, after_ref[total : total + 1, :nx], 0.0)
    image_up = image_ref[pl.ds(jnp.maximum(start - 1, 0), 1), :]
    image_down = image_ref[pl.ds(jnp.minimum(start + count, total - 1), 1), :]
    row = lax.broadcasted_iota(jnp.int32, (count, nx), 0)
    column = lax.broadcasted_iota(jnp.int32, (count, nx), 1)

    def above(values, edge):
        return jnp.where(row == 0, edge, pltpu.roll(values, 1, 0))

    def below(values, edge):
        return jnp.where(row == count - 1, edge, pltpu.roll(values, count - 1, 0))

    return weight_up, weight_down, image_up, image_down, column, above, below


def smooth_kernel(
    image_ref, own_ref, even_ref, odd_ref, weight_ref, weight_even_ref, weight_odd_ref,
    before_ref, after_ref, out_ref, sums_ref,
):
    nx = image_ref.shape[1] // 2
    weight, weight_even, weight_odd = weight_ref[...], weight_even_ref[...], weight_odd_ref[...]
    weight_up, weight_down, image_up, image_down, column, above, below = neighbours(
        image_ref, weight, before_ref, after_ref
    )
    weight_left = jnp.where(column == 0, 0.0, pltpu.roll(weight, 1, 1))
    weight_right = jnp.where(column == nx - 1, 0.0, pltpu.roll(weight, nx - 1, 1))
    weight_above, weight_below = above(weight, weight_up), below(weight, weight_down)
    squares = curvature = 0.0
    for part in range(2):
        lanes = slice(part * nx, (part + 1) * nx)
        here = own_ref[:, lanes]
        flux = weight_even * (here - even_ref[:, lanes]) + weight_odd * (here - odd_ref[:, lanes])
        flux += weight_above * (here - above(here, image_up[:, lanes]))
        flux += weight_below * (here - below(here, image_down[:, lanes]))
        flux += weight_left * (here - pltpu.roll(here, 1, 1))
        flux += weight_right * (here - pltpu.roll(here, nx - 1, 1))
        result = reg_strength * (weight * flux) + damping * here
        out_ref[:, lanes] = result
        squares += here * here
        curvature += here * result
    norm, energy = jnp.sum(squares), jnp.sum(curvature)
    lane = lax.broadcasted_iota(jnp.int32, sums_ref.shape, 1)
    sums_ref[...] = jnp.where(lane == 0, norm, jnp.where(lane == 1, energy, 0.0))


def update_kernel(images, own_ref, smooth_ref, *refs):
    image_refs, sums_refs, (field_ref, residual_ref) = refs[:images], refs[images:-2], refs[-2:]
    sums = sums_refs[0][0:1, :]
    for ref in sums_refs[1:]:
        sums = sums + ref[0:1, :]
    alpha = sums[:, 0:1] / sums[:, 1:2]
    here = own_ref[...]
    image = smooth_ref[...]
    for ref in image_refs:
        image = image + ref[...]
    field_ref[...] = alpha * here
    residual_ref[...] = here - alpha * image


def call(kernel, outs, specs, out_specs, scratch=(), flops=0, nbytes=0, limit=small_vmem):
    return pl.pallas_call(
        kernel,
        out_shape=outs,
        in_specs=specs,
        out_specs=out_specs,
        scratch_shapes=scratch,
        compiler_params=pltpu.CompilerParams(vmem_limit_bytes=limit),
        cost_estimate=pl.CostEstimate(flops=flops, bytes_accessed=nbytes, transcendentals=0),
    )


def shape(dims, dtype=f32):
    return jax.ShapeDtypeStruct(dims, dtype)


def exchange(values, axis, step):
    return lax.ppermute(values, axis, [(i, i ^ step) for i in range(lax.axis_size(axis))])


def powers(axis):
    return [1 << i for i in range(lax.axis_size(axis).bit_length() - 1)]


def from_others(values, axis):
    count = lax.axis_size(axis)
    return [
        lax.ppermute(values, axis, [(i, (i + shift) % count) for i in range(count)]) for shift in range(1, count)
    ]


def on_device(kspace_data, coil_maps, smooth_weight, kernel_cols, kernel_rows, tile_index, caipi_cycle):
    profiles, data, weight = coil_maps[0, 0], kspace_data[0], smooth_weight[0, 0]
    coils, ny, width = profiles.shape
    nx = width // 2
    blocks = tile_index.shape[0]
    samples, ty = kernel_rows.shape
    sb = samples // blocks
    count = weight.shape[0]
    rows, groups = lax.axis_size("row"), lax.axis_size("grp")
    table = jnp.asarray(dft_table(ny))
    wide = blocks * ty
    w_shape = (blocks, 2 * sb, nx)
    row_flops = 2 * 3 * coils * wide * ny * width
    col_flops = 2 * 3 * coils * ty * blocks * (2 * sb) * width
    dma = pltpu.SemaphoreType.DMA
    x_shape = pltpu.VMEM((coils, wide, width), bf16)

    inputs = [tile_index, table, kernel_cols.T, kernel_rows.T, data, weight, profiles]
    fetched = [
        pltpu.SMEM(tile_index.shape, tile_index.dtype),
        *[pltpu.VMEM(x.shape, x.dtype) for x in inputs[1:4]],
    ]
    kept = call(
        functools.partial(tables_kernel, coils, blocks),
        [
            pltpu.VMEM(w_shape, bf16),
            pltpu.VMEM(w_shape, bf16),
            pltpu.VMEM((wide, 3 * ny), bf16),
            pltpu.VMEM((ny, 3 * wide), bf16),
            pltpu.VMEM((blocks, ty, 2 * sb), f32),
            pltpu.VMEM(profiles.shape, bf16),
            pltpu.VMEM(weight.shape, f32),
            pltpu.VMEM((2 * blocks, sb), f32),
            pltpu.VMEM(data.shape, f32),
        ],
        [pl.BlockSpec(memory_space=pltpu.SMEM)] + [HBM] * len(inputs),
        [VMEM] * 9,
        [*fetched, pltpu.VMEM((coils, ny // 2, width), bf16), dma((len(inputs) + 1,))],
        col_flops,
        limit=large_vmem,
    )(caipi_cycle, *(pltpu.with_memory_space_constraint(x, pltpu.HBM) for x in inputs))
    whigh, wlow, fwd, adj, row_weight, coil, weight, phases, data = (
        pltpu.with_memory_space_constraint(x, pltpu.VMEM) for x in kept
    )
    partial = call(
        functools.partial(rhs_kernel, coils, blocks),
        shape((ny + 8, width)),
        [VMEM] * 8,
        VMEM,
        [x_shape, x_shape],
        row_flops + col_flops,
        limit=large_vmem,
    )(phases, row_weight, whigh, wlow, adj, coil, data, weight)

    received = from_others(partial, "row")
    even_pairs = [(i, i ^ 1) for i in range(groups) if i ^ 1 < groups]
    odd_pairs = []
    for i in range(1, groups - 1, 2):
        odd_pairs += [(i, i + 1), (i + 1, i)]
    weights = [lax.ppermute(weight, "grp", pairs) for pairs in (even_pairs, odd_pairs)]
    folded, image, mine = call(
        functools.partial(sum_kernel, ny),
        [shape((ny, width)), shape((ny, width)), shape((count, width))],
        [VMEM] * (1 + len(received)),
        [VMEM] * 3,
    )(partial, *received)
    others = [lax.ppermute(mine, "grp", pairs) for pairs in (even_pairs, odd_pairs)]

    predicted = call(
        functools.partial(predict_kernel, coils, blocks),
        shape((blocks, coils, 2 * sb)),
        [VMEM] * 7,
        VMEM,
        [pltpu.VMEM((blocks, 2, coils * ty, nx), bf16)] * 2,
        row_flops + col_flops,
        limit=large_vmem,
    )(phases, row_weight, folded, fwd, coil, whigh, wlow)

    predicted = [predicted, *[exchange(predicted, "band", step) for step in range(lax.axis_size("band") - 1, 0, -1)]]
    smoothed, sums = call(
        smooth_kernel,
        [shape((count, width)), shape((8, 128))],
        [VMEM] * 9,
        [VMEM, VMEM],
    )(image, mine, *others, weight, *weights, received[0], received[-1])
    sums = [sums, *[exchange(sums, "band", step) for step in range(1, lax.axis_size("band"))]]
    collapsed, sums = call(
        functools.partial(collapse_kernel, len(predicted)),
        [shape(predicted[0].shape), shape((8, 128))],
        [VMEM] * (len(predicted) + len(sums)),
        [VMEM, VMEM],
    )(*predicted, *sums)
    steps = powers("grp")
    for step in steps[:-1]:
        sums = sums + exchange(sums, "grp", step)

    kept = call(
        functools.partial(spread_kernel, coils, blocks),
        [x_shape, x_shape],
        [VMEM] * 5,
        [VMEM] * 2,
        (),
        col_flops,
        limit=large_vmem,
    )(phases, row_weight, whigh, wlow, collapsed)
    xhigh, xlow = (pltpu.with_memory_space_constraint(x, pltpu.VMEM) for x in kept)

    def add_rows(first, last, *before):
        return call(
            functools.partial(rows_kernel, first, last),
            shape((ny, width)),
            [VMEM] * (4 + len(before)),
            VMEM,
            (),
            row_flops * (last - first) // coils,
            limit=large_vmem,
        )(adj, coil, xhigh, xlow, *before)

    unfinished = add_rows(0, coils, sums)
    sums = sums + exchange(sums, "grp", steps[-1])
    halves = call(
        cut_kernel,
        [shape((count, width))] * 2 if rows == 2 else [shape((ny, width))],
        [VMEM] * 2,
        [VMEM] * (2 if rows == 2 else 1),
        [pltpu.VMEM((ny, width), f32)],
    )(sums, unfinished)
    if rows == 2:
        images = [halves[0], exchange(halves[1], "row", 1)]
    else:
        images = [lax.psum_scatter(halves[0], "row", scatter_dimension=0, tiled=True)]
    all_sums = [sums, *from_others(sums, "row")]
    solution_field, residual = call(
        functools.partial(update_kernel, len(images)),
        [shape((count, width))] * 2,
        [VMEM] * (2 + len(images) + len(all_sums)),
        [VMEM, VMEM],
    )(mine, smoothed, *images, *all_sums)
    return solution_field[None, None], residual[None, None]


def solution(mesh):
    return jax.shard_map(
        on_device,
        mesh=mesh,
        in_specs=(
            P("grp", "row", None, None),
            P("band", "grp", "row", None, None),
            P("band", "grp", "row", None),
            P(),
            P(),
            P(),
            P("band"),
        ),
        out_specs=(P("band", "grp", "row", None), P("band", "grp", "row", None)),
        check_vma=False,
    )
```

```python
import functools
import math

import jax
import jax.numpy as jnp
import ml_dtypes
import numpy as np
from jax import lax
from jax.experimental import pallas as pl
from jax.experimental.pallas import tpu as pltpu
from jax.sharding import PartitionSpec as P

reg_strength = 0.5
damping = 1.0
f32 = jnp.float32
bf16 = jnp.bfloat16
VMEM = pl.BlockSpec(memory_space=pltpu.VMEM)
HBM = pl.BlockSpec(memory_space=pltpu.HBM)
TN = (((0,), (0,)), ((), ()))
NT = (((1,), (1,)), ((), ()))
large_vmem = 20 * 1024 * 1024
small_vmem = 8 * 1024 * 1024


def dft_table(length):
    index = np.arange(length)
    angle = (index[:, None] * index[None, :] % length) * (2.0 * np.pi / length)
    parts = []
    for part in (np.cos(angle) / math.sqrt(length), -np.sin(angle) / math.sqrt(length)):
        high = part.astype(ml_dtypes.bfloat16)
        low = (part - high.astype(np.float64)).astype(ml_dtypes.bfloat16)
        parts += [high, low]
    return np.concatenate(parts, axis=0)


def split(values):
    high = values.astype(bf16)
    return high, (values - high.astype(f32)).astype(bf16)


def matmul(left, right):
    return jnp.dot(left, right, preferred_element_type=f32)


def quarter_turn(cycle, block):
    turn = lax.rem(cycle * block, 4)
    one, zero = jnp.float32(1.0), jnp.float32(0.0)
    cosine = jnp.where(turn == 0, one, zero) - jnp.where(turn == 2, one, zero)
    sine = jnp.where(turn == 1, one, zero) - jnp.where(turn == 3, one, zero)
    return cosine, sine


def phase_of(phase_ref, block):
    return phase_ref[2 * block : 2 * block + 1, :], phase_ref[2 * block + 1 : 2 * block + 2, :]


def spread(values, row_weight, whigh, wlow, xhigh, xlow, k, coils, ty):
    weighted = values[:, None, :] * row_weight[None, :, :]
    parts = split(weighted.reshape(coils * ty, values.shape[1]))
    sb = values.shape[1] // 2
    vhigh, vlow = (
        jnp.concatenate([part, jnp.concatenate([part[:, sb:], -part[:, :sb]], axis=1)], axis=0) for part in parts
    )
    rows = matmul(
        jnp.concatenate([vhigh, vlow, vhigh], axis=1),
        jnp.concatenate([whigh, whigh, wlow], axis=0),
    )
    high, low = split(rows)
    there, nx = slice(k * ty, (k + 1) * ty), rows.shape[1]
    for part in range(2):
        for c in range(coils):
            here = slice((part * coils + c) * ty, (part * coils + c + 1) * ty)
            xhigh[c, there, part * nx : (part + 1) * nx] = high[here]
            xlow[c, there, part * nx : (part + 1) * nx] = low[here]


def mirror(rows):
    left = lax.broadcasted_iota(jnp.int32, (rows, rows), 0)
    right = lax.broadcasted_iota(jnp.int32, (rows, rows), 1)
    return (lax.rem(left + right, rows) == 0).astype(f32).astype(bf16)


def mirrored(values):
    high, rest = split(values)
    low = (values - high.astype(f32) - rest.astype(f32)).astype(bf16)
    order = mirror(values.shape[0])
    return matmul(order, high) + (matmul(order, rest) + matmul(order, low))


def with_first(first, values):
    columns = values.shape[1]
    edge = lax.broadcasted_iota(jnp.int32, (8, columns), 0) == 0
    top = jnp.where(edge, first[:8], values[:8])
    return jnp.concatenate([top, values[8:]], axis=0)


def back_rows(adj, xhigh, xlow, coil, first, last):
    ny, nx = adj.shape[0], xhigh.shape[2] // 2
    half = ny // 2
    sums = [None] * 4
    for c in range(first, last):
        high, low = xhigh[c], xlow[c]
        folded = matmul(adj[...], jnp.concatenate([high, high, low], axis=0))
        even_real, even_imag = folded[:half, :nx], folded[:half, nx:]
        odd_real, odd_imag = folded[half:, :nx], folded[half:, nx:]
        lower = with_first(even_real, even_real - odd_imag), with_first(even_imag, even_imag + odd_real)
        upper = with_first(odd_real, even_real + odd_imag), with_first(odd_imag, even_imag - odd_real)
        for i, (real, imag) in enumerate((lower, upper)):
            here = slice(i * half, (i + 1) * half)
            coil_real = coil[c, here, :nx].astype(f32)
            coil_imag = coil[c, here, nx:].astype(f32)
            terms = coil_real * real + coil_imag * imag, coil_real * imag - coil_imag * real
            for j, term in enumerate(terms):
                sums[2 * i + j] = term if c == first else sums[2 * i + j] + term
    return jnp.concatenate(sums[:2], axis=1), jnp.concatenate(sums[2:], axis=1)


def tables_kernel(
    coils, blocks, cycle_ref, tile_any, table_any, cols_any, rows_any, data_any, weight_any, coil_any,
    whigh, wlow, fwd, adj, row_weight_ref, coil, weight_ref, phase_ref, data_ref,
    tile_ref, table_ref, cols_ref, rows_ref, upper, sems,
):
    ny = table_ref.shape[1]
    half = ny // 2
    ty, tx = rows_ref.shape[0], cols_ref.shape[0]
    sb = rows_ref.shape[1] // blocks
    moves = [
        (tile_any, tile_ref),
        (table_any, table_ref),
        (cols_any, cols_ref),
        (rows_any, rows_ref),
        (data_any, data_ref),
        (weight_any, weight_ref),
        (coil_any.at[:, half:, :], upper),
        (coil_any.at[:, :half, :], coil.at[:, :half, :]),
    ]
    fetches = [pltpu.make_async_copy(source, target, sems.at[i]) for i, (source, target) in enumerate(moves)]
    for fetch in fetches:
        fetch.start()
    for fetch in fetches[:-3]:
        fetch.wait()

    first = lax.broadcasted_iota(jnp.int32, (ty, half), 1) == 0
    for k in range(blocks):
        top = pl.multiple_of((tile_ref[k] // (ny // tx)) * ty, ty)
        here = slice(k * ty, (k + 1) * ty)
        for i in range(2):
            real = table_ref[pl.ds(i * ny + top, ty), :].astype(f32)
            imag = table_ref[pl.ds((2 + i) * ny + top, ty), :].astype(f32)
            odd = jnp.where(first, real[:, half:], -imag[:, :half])
            row = jnp.concatenate([real[:, :half], odd], axis=1).astype(bf16)
            for place in (0, 2) if i == 0 else (1,):
                fwd[here, place * ny : (place + 1) * ny] = row
    wide = blocks * ty
    for i in range(2):
        turned = fwd[:, i * ny : (i + 1) * ny].astype(f32).T.astype(bf16)
        for place in (0, 2) if i == 0 else (1,):
            adj[:, place * wide : (place + 1) * wide] = turned

    for k in range(blocks):
        left = pl.multiple_of(lax.rem(tile_ref[k], ny // tx) * tx, tx)
        chosen = [table_ref[pl.ds(i * ny + left, tx), :] for i in (0, 1, 2, 3)]
        stacked = jnp.concatenate(
            [jnp.concatenate([chosen[0], chosen[2]], axis=1), jnp.concatenate([chosen[1], chosen[3]], axis=1)], axis=0
        )
        here = slice(k * sb, (k + 1) * sb)
        cols = cols_ref[:, here]
        mixed = lax.dot_general(
            jnp.concatenate([cols, cols], axis=0), stacked, TN, preferred_element_type=f32
        )
        for ref, part in zip((whigh, wlow), split(mixed)):
            ref[k, :sb, :] = part[:, :ny]
            ref[k, sb:, :] = part[:, ny:]
        turned = rows_ref[:, here].astype(f32)
        row_weight = jnp.concatenate([turned, turned], axis=1)
        row_weight_ref[k] = row_weight
        for i, part in enumerate(quarter_turn(cycle_ref[0], k)):
            phase_ref[2 * k + i : 2 * k + i + 1, :] = jnp.full((1, sb), part, f32)
    for fetch in fetches[-3:-1]:
        fetch.wait()
    order = mirror(half)
    for c in range(coils):
        coil[c, half:, :] = matmul(order, upper[c]).astype(bf16)
    fetches[-1].wait()


def rhs_kernel(
    coils, blocks, phase_ref, row_weight_ref, whigh, wlow, adj, coil, data_ref, weight_ref, part_ref, xhigh, xlow
):
    ny = adj.shape[0]
    half = ny // 2
    ty = row_weight_ref.shape[1]
    sb = row_weight_ref.shape[2] // 2
    for k in range(blocks):
        here = slice(k * sb, (k + 1) * sb)
        cosine, sine = phase_of(phase_ref, k)
        real, imag = data_ref[:, 0, here], data_ref[:, 1, here]
        values = jnp.concatenate([cosine * real + sine * imag, cosine * imag - sine * real], axis=1)
        spread(values, row_weight_ref[k], whigh[k], wlow[k], xhigh, xlow, k, coils, ty)
    lower_rows, upper_rows = back_rows(adj, xhigh, xlow, coil, 0, coils)
    part_ref[:half, :] = lower_rows
    part_ref[half:ny, :] = upper_rows
    count = weight_ref.shape[0]
    edge = jnp.concatenate([weight_ref[0:1, :], weight_ref[count - 1 : count, :]], axis=0)
    edge = jnp.concatenate([edge, jnp.zeros((6, edge.shape[1]), f32)], axis=0)
    part_ref[ny:, :] = jnp.concatenate([edge, jnp.zeros_like(edge)], axis=1)


def sum_kernel(ny, *refs):
    parts, (folded_ref, image_ref, mine_ref) = refs[:-3], refs[-3:]
    total = parts[0][:ny, :]
    for part in parts[1:]:
        total = total + part[:ny, :]
    folded_ref[...] = total
    image_ref[: ny // 2, :] = total[: ny // 2]
    image_ref[ny // 2 :, :] = mirrored(total[ny // 2 :])
    count = mine_ref.shape[0]
    mine_ref[...] = image_ref[pl.ds(pl.multiple_of(lax.axis_index("row") * count, count), count), :]


def predict_kernel(
    coils, blocks, phase_ref, row_weight_ref, image_ref, fwd, coil, whigh, wlow, out_ref, thigh, tlow
):
    ny, nx = image_ref.shape[0], image_ref.shape[1] // 2
    half = ny // 2
    ty = row_weight_ref.shape[1]
    sb = row_weight_ref.shape[2] // 2
    for c in range(coils):
        products = []
        for i in range(2):
            here = slice(i * half, (i + 1) * half)
            coil_real = coil[c, here, :nx].astype(f32)
            coil_imag = coil[c, here, nx:].astype(f32)
            image_real, image_imag = image_ref[here, :nx], image_ref[here, nx:]
            products.append(coil_real * image_real - coil_imag * image_imag)
            products.append(coil_real * image_imag + coil_imag * image_real)
        lower_real, lower_imag, upper_real, upper_imag = products
        even = [with_first(lower_real, lower_real + upper_real), with_first(lower_imag, lower_imag + upper_imag)]
        odd = [with_first(upper_real, lower_imag - upper_imag), with_first(upper_imag, upper_real - lower_real)]
        folded = jnp.concatenate([jnp.concatenate(even, axis=1), jnp.concatenate(odd, axis=1)], axis=0)
        high, low = split(folded)
        grid = matmul(fwd[...], jnp.concatenate([high, high, low], axis=0))
        for ref, part in zip((thigh, tlow), split(grid)):
            ref[:, 0, c * ty : (c + 1) * ty, :] = part[:, :nx].reshape(blocks, ty, nx)
            ref[:, 1, c * ty : (c + 1) * ty, :] = part[:, nx:].reshape(blocks, ty, nx)
    for k in range(blocks):
        left_high, left_low = (ref[k].reshape(2 * coils * ty, nx) for ref in (thigh, tlow))
        right_high = whigh[k]
        mixed = lax.dot_general(
            jnp.concatenate([left_high, left_low, left_high], axis=1),
            jnp.concatenate([right_high, right_high, wlow[k]], axis=1),
            NT,
            preferred_element_type=f32,
        )
        of_real, of_imag = mixed[: coils * ty], mixed[coils * ty :]
        product = jnp.concatenate(
            [of_real[:, :sb] - of_imag[:, sb:], of_real[:, sb:] + of_imag[:, :sb]], axis=1
        )
        summed = jnp.sum(product.reshape(coils, ty, 2 * sb) * row_weight_ref[k][None, :, :], axis=1)
        real, imag = summed[:, :sb], summed[:, sb:]
        cosine, sine = phase_of(phase_ref, k)
        out_ref[k] = jnp.concatenate([cosine * real - sine * imag, sine * real + cosine * imag], axis=1)


def collapse_kernel(bands, *refs):
    parts, sums_refs, (out_ref, out_sums_ref) = refs[:bands], refs[bands:-2], refs[-2:]
    total = parts[0][...]
    for part in parts[1:]:
        total = total + part[...]
    out_ref[...] = total
    sums = sums_refs[0][...]
    for ref in sums_refs[1:]:
        sums = sums + ref[...]
    lane = lax.broadcasted_iota(jnp.int32, sums.shape, 1)
    squares = jnp.sum(jnp.sum(total * total, axis=0))
    out_sums_ref[...] = jnp.where(lane == 1, sums + squares, sums)


def spread_kernel(coils, blocks, phase_ref, row_weight_ref, whigh, wlow, collapsed_ref, xhigh, xlow):
    ty = row_weight_ref.shape[1]
    sb = row_weight_ref.shape[2] // 2
    for k in range(blocks):
        cosine, sine = phase_of(phase_ref, k)
        real, imag = collapsed_ref[k, :, :sb], collapsed_ref[k, :, sb:]
        values = jnp.concatenate([cosine * real + sine * imag, cosine * imag - sine * real], axis=1)
        spread(values, row_weight_ref[k], whigh[k], wlow[k], xhigh, xlow, k, coils, ty)


def rows_kernel(first, last, adj, coil, xhigh, xlow, *refs):
    out_ref = refs[-1]
    half = out_ref.shape[0] // 2
    for i, rows in enumerate(back_rows(adj, xhigh, xlow, coil, first, last)):
        here = slice(i * half, (i + 1) * half)
        out_ref[here, :] = rows + refs[0][here, :] if first else rows


def cut_kernel(count, sums_ref, folded_ref, *refs):
    *out_refs, whole = refs
    total = whole.shape[0]
    half = total // 2
    whole[:half, :] = folded_ref[:half, :]
    whole[half:, :] = mirrored(folded_ref[half:, :])
    for shift, out_ref in enumerate(out_refs):
        start = lax.rem(lax.axis_index("row") + shift, total // count) * count
        out_ref[:count, :] = whole[pl.ds(pl.multiple_of(start, count), count), :]
        if out_ref.shape[0] > count:
            out_ref[count:, :] = jnp.concatenate([sums_ref[...]] * (whole.shape[1] // sums_ref.shape[1]), axis=1)


def neighbours(image_ref, weight, before_ref, after_ref):
    count, nx = weight.shape
    total = image_ref.shape[0]
    place = lax.axis_index("row")
    start = place * count
    weight_up = jnp.where(place > 0, before_ref[total + 1 : total + 2, :nx], 0.0)
    weight_down = jnp.where(place < total // count - 1, after_ref[total : total + 1, :nx], 0.0)
    image_up = image_ref[pl.ds(jnp.maximum(start - 1, 0), 1), :]
    image_down = image_ref[pl.ds(jnp.minimum(start + count, total - 1), 1), :]
    row = lax.broadcasted_iota(jnp.int32, (count, nx), 0)
    column = lax.broadcasted_iota(jnp.int32, (count, nx), 1)

    def above(values, edge):
        return jnp.where(row == 0, edge, pltpu.roll(values, 1, 0))

    def below(values, edge):
        return jnp.where(row == count - 1, edge, pltpu.roll(values, count - 1, 0))

    return weight_up, weight_down, image_up, image_down, column, above, below


def smooth_kernel(
    image_ref, own_ref, even_ref, odd_ref, weight_ref, weight_even_ref, weight_odd_ref,
    before_ref, after_ref, out_ref, sums_ref,
):
    nx = image_ref.shape[1] // 2
    weight, weight_even = weight_ref[...], weight_even_ref[...]
    group = lax.axis_index("grp")
    inside = jnp.logical_and(group > 0, group < lax.axis_size("grp") - 1)
    weight_odd = jnp.where(inside, weight_odd_ref[...], 0.0)
    weight_up, weight_down, image_up, image_down, column, above, below = neighbours(
        image_ref, weight, before_ref, after_ref
    )
    weight_left = jnp.where(column == 0, 0.0, pltpu.roll(weight, 1, 1))
    weight_right = jnp.where(column == nx - 1, 0.0, pltpu.roll(weight, nx - 1, 1))
    weight_above, weight_below = above(weight, weight_up), below(weight, weight_down)
    squares = curvature = 0.0
    for part in range(2):
        lanes = slice(part * nx, (part + 1) * nx)
        here = own_ref[:, lanes]
        flux = weight_even * (here - even_ref[:, lanes]) + weight_odd * (here - odd_ref[:, lanes])
        flux += weight_above * (here - above(here, image_up[:, lanes]))
        flux += weight_below * (here - below(here, image_down[:, lanes]))
        flux += weight_left * (here - pltpu.roll(here, 1, 1))
        flux += weight_right * (here - pltpu.roll(here, nx - 1, 1))
        result = reg_strength * (weight * flux) + damping * here
        out_ref[:, lanes] = result
        squares += here * here
        curvature += here * result
    norm, energy = jnp.sum(squares), jnp.sum(curvature)
    lane = lax.broadcasted_iota(jnp.int32, sums_ref.shape, 1)
    sums_ref[...] = jnp.where(lane == 0, norm, jnp.where(lane == 1, energy, 0.0))


def update_kernel(images, own_ref, smooth_ref, *refs):
    image_refs, sums_refs, (field_ref, residual_ref) = refs[:images], refs[images:-2], refs[-2:]
    count = smooth_ref.shape[0]
    sums = sums_refs[0][0:1, :]
    for ref in sums_refs[1:]:
        sums = sums + ref[0:1, :]
    for ref in image_refs:
        if ref.shape[0] > count:
            sums = sums + ref[count : count + 1, : sums.shape[1]]
    alpha = sums[:, 0:1] / sums[:, 1:2]
    here = own_ref[...]
    image = smooth_ref[...]
    for ref in image_refs:
        image = image + ref[:count, :]
    field_ref[...] = alpha * here
    residual_ref[...] = here - alpha * image


def call(kernel, outs, specs, out_specs, scratch=(), flops=0, nbytes=0, limit=small_vmem):
    return pl.pallas_call(
        kernel,
        out_shape=outs,
        in_specs=specs,
        out_specs=out_specs,
        scratch_shapes=scratch,
        compiler_params=pltpu.CompilerParams(vmem_limit_bytes=limit),
        cost_estimate=pl.CostEstimate(flops=flops, bytes_accessed=nbytes, transcendentals=0),
    )


def shape(dims, dtype=f32):
    return jax.ShapeDtypeStruct(dims, dtype)


def exchange(values, axis, step):
    return lax.ppermute(values, axis, [(i, i ^ step) for i in range(lax.axis_size(axis))])


def powers(axis):
    return [1 << i for i in range(lax.axis_size(axis).bit_length() - 1)]


def from_others(values, axis):
    count = lax.axis_size(axis)
    return [
        lax.ppermute(values, axis, [(i, (i + shift) % count) for i in range(count)]) for shift in range(1, count)
    ]


def on_device(kspace_data, coil_maps, smooth_weight, kernel_cols, kernel_rows, tile_index, caipi_cycle):
    profiles, data, weight = coil_maps[0, 0], kspace_data[0], smooth_weight[0, 0]
    coils, ny, width = profiles.shape
    nx = width // 2
    blocks = tile_index.shape[0]
    samples, ty = kernel_rows.shape
    sb = samples // blocks
    count = weight.shape[0]
    rows, groups = lax.axis_size("row"), lax.axis_size("grp")
    table = jnp.asarray(dft_table(ny))
    wide = blocks * ty
    w_shape = (blocks, 2 * sb, nx)
    row_flops = 2 * 3 * coils * wide * ny * width
    col_flops = 2 * 3 * coils * ty * blocks * (2 * sb) * width
    dma = pltpu.SemaphoreType.DMA
    x_shape = pltpu.VMEM((coils, wide, width), bf16)

    inputs = [tile_index, table, kernel_cols.T, kernel_rows.T, data, weight, profiles]
    fetched = [
        pltpu.SMEM(tile_index.shape, tile_index.dtype),
        *[pltpu.VMEM(x.shape, x.dtype) for x in inputs[1:4]],
    ]
    kept = call(
        functools.partial(tables_kernel, coils, blocks),
        [
            pltpu.VMEM(w_shape, bf16),
            pltpu.VMEM(w_shape, bf16),
            pltpu.VMEM((wide, 3 * ny), bf16),
            pltpu.VMEM((ny, 3 * wide), bf16),
            pltpu.VMEM((blocks, ty, 2 * sb), f32),
            pltpu.VMEM(profiles.shape, bf16),
            pltpu.VMEM(weight.shape, f32),
            pltpu.VMEM((2 * blocks, sb), f32),
            pltpu.VMEM(data.shape, f32),
        ],
        [pl.BlockSpec(memory_space=pltpu.SMEM)] + [HBM] * len(inputs),
        [VMEM] * 9,
        [*fetched, pltpu.VMEM((coils, ny // 2, width), bf16), dma((len(inputs) + 1,))],
        col_flops,
        limit=large_vmem,
    )(caipi_cycle, *(pltpu.with_memory_space_constraint(x, pltpu.HBM) for x in inputs))
    whigh, wlow, fwd, adj, row_weight, coil, weight, phases, data = (
        pltpu.with_memory_space_constraint(x, pltpu.VMEM) for x in kept
    )
    partial = call(
        functools.partial(rhs_kernel, coils, blocks),
        shape((ny + 8, width)),
        [VMEM] * 8,
        VMEM,
        [x_shape, x_shape],
        row_flops + col_flops,
        limit=large_vmem,
    )(phases, row_weight, whigh, wlow, adj, coil, data, weight)

    received = from_others(partial, "row")
    even_pairs = [(i, i ^ 1) for i in range(groups) if i ^ 1 < groups]
    ends = (0, groups - 1)
    beyond = [group if group in ends else ((group - 1) ^ 1) + 1 for group in range(groups)]
    odd_pairs = [
        (group * rows + row, beyond[group] * rows + ((row + 1) % rows if group in ends else row))
        for group in range(groups)
        for row in range(rows)
    ]
    beside = (("grp", even_pairs), (("grp", "row"), odd_pairs))
    weights = [lax.ppermute(weight, axes, pairs) for axes, pairs in beside]
    folded, image, mine = call(
        functools.partial(sum_kernel, ny),
        [shape((ny, width)), shape((ny, width)), shape((count, width))],
        [VMEM] * (1 + len(received)),
        [VMEM] * 3,
    )(partial, *received)
    others = [lax.ppermute(mine, axes, pairs) for axes, pairs in beside]

    predicted = call(
        functools.partial(predict_kernel, coils, blocks),
        shape((blocks, coils, 2 * sb)),
        [VMEM] * 7,
        VMEM,
        [pltpu.VMEM((blocks, 2, coils * ty, nx), bf16)] * 2,
        row_flops + col_flops,
        limit=large_vmem,
    )(phases, row_weight, folded, fwd, coil, whigh, wlow)

    predicted = [predicted, *[exchange(predicted, "band", step) for step in range(lax.axis_size("band") - 1, 0, -1)]]
    smoothed, sums = call(
        smooth_kernel,
        [shape((count, width)), shape((8, 128))],
        [VMEM] * 9,
        [VMEM, VMEM],
    )(image, mine, *others, weight, *weights, received[0], received[-1])
    sums = [sums, *[exchange(sums, "band", step) for step in range(1, lax.axis_size("band"))]]
    collapsed, sums = call(
        functools.partial(collapse_kernel, len(predicted)),
        [shape(predicted[0].shape), shape((8, 128))],
        [VMEM] * (len(predicted) + len(sums)),
        [VMEM, VMEM],
    )(*predicted, *sums)
    steps = powers("grp")
    for step in steps[:-1]:
        sums = sums + exchange(sums, "grp", step)

    kept = call(
        functools.partial(spread_kernel, coils, blocks),
        [x_shape, x_shape],
        [VMEM] * 5,
        [VMEM] * 2,
        (),
        col_flops,
        limit=large_vmem,
    )(phases, row_weight, whigh, wlow, collapsed)
    xhigh, xlow = (pltpu.with_memory_space_constraint(x, pltpu.VMEM) for x in kept)

    def add_rows(first, last, *before):
        return call(
            functools.partial(rows_kernel, first, last),
            shape((ny, width)),
            [VMEM] * (4 + len(before)),
            VMEM,
            (),
            row_flops * (last - first) // coils,
            limit=large_vmem,
        )(adj, coil, xhigh, xlow, *before)

    unfinished = add_rows(0, coils, sums)
    sums = sums + exchange(sums, "grp", steps[-1])
    cuts = [(count, width), (count + sums.shape[0], width)] if rows == 2 else [(ny, width)]
    halves = call(
        functools.partial(cut_kernel, count if rows == 2 else ny),
        [shape(cut) for cut in cuts],
        [VMEM] * 2,
        [VMEM] * len(cuts),
        [pltpu.VMEM((ny, width), f32)],
    )(sums, unfinished)
    if rows == 2:
        images = [halves[0], exchange(halves[1], "row", 1)]
        all_sums = [sums]
    else:
        images = [lax.psum_scatter(halves[0], "row", scatter_dimension=0, tiled=True)]
        all_sums = [sums, *from_others(sums, "row")]
    solution_field, residual = call(
        functools.partial(update_kernel, len(images)),
        [shape((count, width))] * 2,
        [VMEM] * (2 + len(images) + len(all_sums)),
        [VMEM, VMEM],
    )(mine, smoothed, *images, *all_sums)
    return solution_field[None, None], residual[None, None]


def solution(mesh):
    return jax.shard_map(
        on_device,
        mesh=mesh,
        in_specs=(
            P("grp", "row", None, None),
            P("band", "grp", "row", None, None),
            P("band", "grp", "row", None),
            P(),
            P(),
            P(),
            P("band"),
        ),
        out_specs=(P("band", "grp", "row", None), P("band", "grp", "row", None)),
        check_vma=False,
    )
```

```python
import functools
import math

import jax
import jax.numpy as jnp
import ml_dtypes
import numpy as np
from jax import lax
from jax.experimental import pallas as pl
from jax.experimental.pallas import tpu as pltpu
from jax.sharding import PartitionSpec as P

reg_strength = 0.5
damping = 1.0
f32 = jnp.float32
bf16 = jnp.bfloat16
VMEM = pl.BlockSpec(memory_space=pltpu.VMEM)
HBM = pl.BlockSpec(memory_space=pltpu.HBM)
TN = (((0,), (0,)), ((), ()))
NT = (((1,), (1,)), ((), ()))
large_vmem = 20 * 1024 * 1024
small_vmem = 8 * 1024 * 1024


def dft_table(length):
    index = np.arange(length)
    angle = (index[:, None] * index[None, :] % length) * (2.0 * np.pi / length)
    parts = []
    for part in (np.cos(angle) / math.sqrt(length), -np.sin(angle) / math.sqrt(length)):
        high = part.astype(ml_dtypes.bfloat16)
        low = (part - high.astype(np.float64)).astype(ml_dtypes.bfloat16)
        parts += [high, low]
    return np.concatenate(parts, axis=0)


def split(values):
    high = values.astype(bf16)
    return high, (values - high.astype(f32)).astype(bf16)


def matmul(left, right):
    return jnp.dot(left, right, preferred_element_type=f32)


def quarter_turn(cycle, block):
    turn = lax.rem(cycle * block, 4)
    one, zero = jnp.float32(1.0), jnp.float32(0.0)
    cosine = jnp.where(turn == 0, one, zero) - jnp.where(turn == 2, one, zero)
    sine = jnp.where(turn == 1, one, zero) - jnp.where(turn == 3, one, zero)
    return cosine, sine


def phase_of(phase_ref, block):
    return phase_ref[2 * block : 2 * block + 1, :], phase_ref[2 * block + 1 : 2 * block + 2, :]


def spread(values, row_weight, whigh, wlow, xhigh, xlow, k, coils, ty):
    weighted = values[:, None, :] * row_weight[None, :, :]
    parts = split(weighted.reshape(coils * ty, values.shape[1]))
    sb = values.shape[1] // 2
    vhigh, vlow = (
        jnp.concatenate([part, jnp.concatenate([part[:, sb:], -part[:, :sb]], axis=1)], axis=0) for part in parts
    )
    rows = matmul(
        jnp.concatenate([vhigh, vlow, vhigh], axis=1),
        jnp.concatenate([whigh, whigh, wlow], axis=0),
    )
    high, low = split(rows)
    there, nx = slice(k * ty, (k + 1) * ty), rows.shape[1]
    for part in range(2):
        for c in range(coils):
            here = slice((part * coils + c) * ty, (part * coils + c + 1) * ty)
            xhigh[c, there, part * nx : (part + 1) * nx] = high[here]
            xlow[c, there, part * nx : (part + 1) * nx] = low[here]


def mirror(rows):
    left = lax.broadcasted_iota(jnp.int32, (rows, rows), 0)
    right = lax.broadcasted_iota(jnp.int32, (rows, rows), 1)
    return (lax.rem(left + right, rows) == 0).astype(f32).astype(bf16)


def mirrored(values):
    high, rest = split(values)
    low = (values - high.astype(f32) - rest.astype(f32)).astype(bf16)
    order = mirror(values.shape[0])
    return matmul(order, high) + (matmul(order, rest) + matmul(order, low))


def with_first(first, values):
    columns = values.shape[1]
    edge = lax.broadcasted_iota(jnp.int32, (8, columns), 0) == 0
    top = jnp.where(edge, first[:8], values[:8])
    return jnp.concatenate([top, values[8:]], axis=0)


def back_rows(adj, xhigh, xlow, coil, first, last):
    ny, nx = adj.shape[0], xhigh.shape[2] // 2
    half = ny // 2
    sums = [None] * 4
    for c in range(first, last):
        high, low = xhigh[c], xlow[c]
        folded = matmul(adj[...], jnp.concatenate([high, high, low], axis=0))
        even_real, even_imag = folded[:half, :nx], folded[:half, nx:]
        odd_real, odd_imag = folded[half:, :nx], folded[half:, nx:]
        lower = with_first(even_real, even_real - odd_imag), with_first(even_imag, even_imag + odd_real)
        upper = with_first(odd_real, even_real + odd_imag), with_first(odd_imag, even_imag - odd_real)
        for i, (real, imag) in enumerate((lower, upper)):
            here = slice(i * half, (i + 1) * half)
            coil_real = coil[c, here, :nx].astype(f32)
            coil_imag = coil[c, here, nx:].astype(f32)
            terms = coil_real * real + coil_imag * imag, coil_real * imag - coil_imag * real
            for j, term in enumerate(terms):
                sums[2 * i + j] = term if c == first else sums[2 * i + j] + term
    return jnp.concatenate(sums[:2], axis=1), jnp.concatenate(sums[2:], axis=1)


def tables_kernel(
    coils, blocks, cycle_ref, tile_any, table_any, cols_any, rows_any, data_any, weight_any, coil_any,
    whigh, wlow, fwd, adj, row_weight_ref, coil, weight_ref, phase_ref, data_ref,
    tile_ref, table_ref, cols_ref, rows_ref, upper, sems,
):
    ny = table_ref.shape[1]
    half = ny // 2
    ty, tx = rows_ref.shape[0], cols_ref.shape[0]
    sb = rows_ref.shape[1] // blocks
    moves = [
        (tile_any, tile_ref),
        (table_any, table_ref),
        (cols_any, cols_ref),
        (rows_any, rows_ref),
        (data_any, data_ref),
        (weight_any, weight_ref),
        (coil_any.at[:, half:, :], upper),
        (coil_any.at[:, :half, :], coil.at[:, :half, :]),
    ]
    fetches = [pltpu.make_async_copy(source, target, sems.at[i]) for i, (source, target) in enumerate(moves)]
    for fetch in fetches:
        fetch.start()
    for fetch in fetches[:-3]:
        fetch.wait()

    first = lax.broadcasted_iota(jnp.int32, (ty, half), 1) == 0
    for k in range(blocks):
        top = pl.multiple_of((tile_ref[k] // (ny // tx)) * ty, ty)
        here = slice(k * ty, (k + 1) * ty)
        for i in range(2):
            real = table_ref[pl.ds(i * ny + top, ty), :].astype(f32)
            imag = table_ref[pl.ds((2 + i) * ny + top, ty), :].astype(f32)
            odd = jnp.where(first, real[:, half:], -imag[:, :half])
            row = jnp.concatenate([real[:, :half], odd], axis=1).astype(bf16)
            for place in (0, 2) if i == 0 else (1,):
                fwd[here, place * ny : (place + 1) * ny] = row
    wide = blocks * ty
    for i in range(2):
        turned = fwd[:, i * ny : (i + 1) * ny].astype(f32).T.astype(bf16)
        for place in (0, 2) if i == 0 else (1,):
            adj[:, place * wide : (place + 1) * wide] = turned

    for k in range(blocks):
        left = pl.multiple_of(lax.rem(tile_ref[k], ny // tx) * tx, tx)
        chosen = [table_ref[pl.ds(i * ny + left, tx), :] for i in (0, 1, 2, 3)]
        stacked = jnp.concatenate(
            [jnp.concatenate([chosen[0], chosen[2]], axis=1), jnp.concatenate([chosen[1], chosen[3]], axis=1)], axis=0
        )
        here = slice(k * sb, (k + 1) * sb)
        cols = cols_ref[:, here]
        mixed = lax.dot_general(
            jnp.concatenate([cols, cols], axis=0), stacked, TN, preferred_element_type=f32
        )
        for ref, part in zip((whigh, wlow), split(mixed)):
            ref[k, :sb, :] = part[:, :ny]
            ref[k, sb:, :] = part[:, ny:]
        turned = rows_ref[:, here].astype(f32)
        row_weight = jnp.concatenate([turned, turned], axis=1)
        row_weight_ref[k] = row_weight
        for i, part in enumerate(quarter_turn(cycle_ref[0], k)):
            phase_ref[2 * k + i : 2 * k + i + 1, :] = jnp.full((1, sb), part, f32)
    for fetch in fetches[-3:-1]:
        fetch.wait()
    order = mirror(half)
    for c in range(coils):
        coil[c, half:, :] = matmul(order, upper[c]).astype(bf16)
    fetches[-1].wait()


def rhs_kernel(
    coils, blocks, phase_ref, row_weight_ref, whigh, wlow, adj, coil, data_ref, weight_ref, part_ref, xhigh, xlow
):
    ny = adj.shape[0]
    half = ny // 2
    ty = row_weight_ref.shape[1]
    sb = row_weight_ref.shape[2] // 2
    for k in range(blocks):
        here = slice(k * sb, (k + 1) * sb)
        cosine, sine = phase_of(phase_ref, k)
        real, imag = data_ref[:, 0, here], data_ref[:, 1, here]
        values = jnp.concatenate([cosine * real + sine * imag, cosine * imag - sine * real], axis=1)
        spread(values, row_weight_ref[k], whigh[k], wlow[k], xhigh, xlow, k, coils, ty)
    lower_rows, upper_rows = back_rows(adj, xhigh, xlow, coil, 0, coils)
    part_ref[:half, :] = lower_rows
    part_ref[half:ny, :] = upper_rows
    count = weight_ref.shape[0]
    edge = jnp.concatenate([weight_ref[0:1, :], weight_ref[count - 1 : count, :]], axis=0)
    edge = jnp.concatenate([edge, jnp.zeros((6, edge.shape[1]), f32)], axis=0)
    part_ref[ny:, :] = jnp.concatenate([edge, jnp.zeros_like(edge)], axis=1)


def sum_kernel(ny, *refs):
    parts, (folded_ref, image_ref, mine_ref) = refs[:-3], refs[-3:]
    total = parts[0][:ny, :]
    for part in parts[1:]:
        total = total + part[:ny, :]
    folded_ref[...] = total
    image_ref[: ny // 2, :] = total[: ny // 2]
    image_ref[ny // 2 :, :] = mirrored(total[ny // 2 :])
    count = mine_ref.shape[0]
    mine_ref[...] = image_ref[pl.ds(pl.multiple_of(lax.axis_index("row") * count, count), count), :]


def predict_kernel(
    coils, blocks, phase_ref, row_weight_ref, image_ref, fwd, coil, whigh, wlow, out_ref, thigh, tlow
):
    ny, nx = image_ref.shape[0], image_ref.shape[1] // 2
    half = ny // 2
    ty = row_weight_ref.shape[1]
    sb = row_weight_ref.shape[2] // 2
    for c in range(coils):
        products = []
        for i in range(2):
            here = slice(i * half, (i + 1) * half)
            coil_real = coil[c, here, :nx].astype(f32)
            coil_imag = coil[c, here, nx:].astype(f32)
            image_real, image_imag = image_ref[here, :nx], image_ref[here, nx:]
            products.append(coil_real * image_real - coil_imag * image_imag)
            products.append(coil_real * image_imag + coil_imag * image_real)
        lower_real, lower_imag, upper_real, upper_imag = products
        even = [with_first(lower_real, lower_real + upper_real), with_first(lower_imag, lower_imag + upper_imag)]
        odd = [with_first(upper_real, lower_imag - upper_imag), with_first(upper_imag, upper_real - lower_real)]
        folded = jnp.concatenate([jnp.concatenate(even, axis=1), jnp.concatenate(odd, axis=1)], axis=0)
        high, low = split(folded)
        grid = matmul(fwd[...], jnp.concatenate([high, high, low], axis=0))
        for ref, part in zip((thigh, tlow), split(grid)):
            ref[:, 0, c * ty : (c + 1) * ty, :] = part[:, :nx].reshape(blocks, ty, nx)
            ref[:, 1, c * ty : (c + 1) * ty, :] = part[:, nx:].reshape(blocks, ty, nx)
    for k in range(blocks):
        left_high, left_low = (ref[k].reshape(2 * coils * ty, nx) for ref in (thigh, tlow))
        right_high = whigh[k]
        mixed = lax.dot_general(
            jnp.concatenate([left_high, left_low, left_high], axis=1),
            jnp.concatenate([right_high, right_high, wlow[k]], axis=1),
            NT,
            preferred_element_type=f32,
        )
        of_real, of_imag = mixed[: coils * ty], mixed[coils * ty :]
        product = jnp.concatenate(
            [of_real[:, :sb] - of_imag[:, sb:], of_real[:, sb:] + of_imag[:, :sb]], axis=1
        )
        summed = jnp.sum(product.reshape(coils, ty, 2 * sb) * row_weight_ref[k][None, :, :], axis=1)
        real, imag = summed[:, :sb], summed[:, sb:]
        cosine, sine = phase_of(phase_ref, k)
        out_ref[k] = jnp.concatenate([cosine * real - sine * imag, sine * real + cosine * imag], axis=1)


def collapse_kernel(*refs):
    parts, (out_ref, sums_ref) = refs[:-2], refs[-2:]
    total = parts[0][...]
    for part in parts[1:]:
        total = total + part[...]
    out_ref[...] = total
    lane = lax.broadcasted_iota(jnp.int32, sums_ref.shape, 1)
    squares = jnp.sum(jnp.sum(total * total, axis=0))
    sums_ref[...] = jnp.where(lane == 1, squares, 0.0)


def spread_kernel(coils, blocks, phase_ref, row_weight_ref, whigh, wlow, collapsed_ref, xhigh, xlow):
    ty = row_weight_ref.shape[1]
    sb = row_weight_ref.shape[2] // 2
    for k in range(blocks):
        cosine, sine = phase_of(phase_ref, k)
        real, imag = collapsed_ref[k, :, :sb], collapsed_ref[k, :, sb:]
        values = jnp.concatenate([cosine * real + sine * imag, cosine * imag - sine * real], axis=1)
        spread(values, row_weight_ref[k], whigh[k], wlow[k], xhigh, xlow, k, coils, ty)


def rows_kernel(first, last, adj, coil, xhigh, xlow, *refs):
    out_ref = refs[-1]
    half = out_ref.shape[0] // 2
    for i, rows in enumerate(back_rows(adj, xhigh, xlow, coil, first, last)):
        here = slice(i * half, (i + 1) * half)
        out_ref[here, :] = rows + refs[0][here, :] if first else rows


def cut_kernel(count, sums_ref, folded_ref, *refs):
    *out_refs, whole = refs
    total = whole.shape[0]
    half = total // 2
    whole[:half, :] = folded_ref[:half, :]
    whole[half:, :] = mirrored(folded_ref[half:, :])
    for shift, out_ref in enumerate(out_refs):
        start = lax.rem(lax.axis_index("row") + shift, total // count) * count
        out_ref[:count, :] = whole[pl.ds(pl.multiple_of(start, count), count), :]
        if out_ref.shape[0] > count:
            out_ref[count:, :] = jnp.concatenate([sums_ref[...]] * (whole.shape[1] // sums_ref.shape[1]), axis=1)


def neighbours(image_ref, weight, before_ref, after_ref):
    count, nx = weight.shape
    total = image_ref.shape[0]
    place = lax.axis_index("row")
    start = place * count
    weight_up = jnp.where(place > 0, before_ref[total + 1 : total + 2, :nx], 0.0)
    weight_down = jnp.where(place < total // count - 1, after_ref[total : total + 1, :nx], 0.0)
    image_up = image_ref[pl.ds(jnp.maximum(start - 1, 0), 1), :]
    image_down = image_ref[pl.ds(jnp.minimum(start + count, total - 1), 1), :]
    row = lax.broadcasted_iota(jnp.int32, (count, nx), 0)
    column = lax.broadcasted_iota(jnp.int32, (count, nx), 1)

    def above(values, edge):
        return jnp.where(row == 0, edge, pltpu.roll(values, 1, 0))

    def below(values, edge):
        return jnp.where(row == count - 1, edge, pltpu.roll(values, count - 1, 0))

    return weight_up, weight_down, image_up, image_down, column, above, below


def smooth_kernel(
    image_ref, own_ref, even_ref, odd_ref, weight_ref, weight_even_ref, weight_odd_ref,
    before_ref, after_ref, out_ref, sums_ref,
):
    nx = image_ref.shape[1] // 2
    weight, weight_even = weight_ref[...], weight_even_ref[...]
    group = lax.axis_index("grp")
    inside = jnp.logical_and(group > 0, group < lax.axis_size("grp") - 1)
    weight_odd = jnp.where(inside, weight_odd_ref[...], 0.0)
    weight_up, weight_down, image_up, image_down, column, above, below = neighbours(
        image_ref, weight, before_ref, after_ref
    )
    weight_left = jnp.where(column == 0, 0.0, pltpu.roll(weight, 1, 1))
    weight_right = jnp.where(column == nx - 1, 0.0, pltpu.roll(weight, nx - 1, 1))
    weight_above, weight_below = above(weight, weight_up), below(weight, weight_down)
    squares = curvature = 0.0
    for part in range(2):
        lanes = slice(part * nx, (part + 1) * nx)
        here = own_ref[:, lanes]
        flux = weight_even * (here - even_ref[:, lanes]) + weight_odd * (here - odd_ref[:, lanes])
        flux += weight_above * (here - above(here, image_up[:, lanes]))
        flux += weight_below * (here - below(here, image_down[:, lanes]))
        flux += weight_left * (here - pltpu.roll(here, 1, 1))
        flux += weight_right * (here - pltpu.roll(here, nx - 1, 1))
        result = reg_strength * (weight * flux) + damping * here
        out_ref[:, lanes] = result
        squares += here * here
        curvature += here * result
    norm, energy = jnp.sum(squares), jnp.sum(curvature)
    lane = lax.broadcasted_iota(jnp.int32, sums_ref.shape, 1)
    sums_ref[...] = jnp.where(lane == 0, norm, jnp.where(lane == 1, energy, 0.0))


def update_kernel(images, own_ref, smooth_ref, *refs):
    image_refs, sums_refs, (field_ref, residual_ref) = refs[:images], refs[images:-2], refs[-2:]
    count = smooth_ref.shape[0]
    sums = sums_refs[0][0:1, :]
    for ref in sums_refs[1:]:
        sums = sums + ref[0:1, :]
    for ref in image_refs:
        if ref.shape[0] > count:
            sums = sums + ref[count : count + 1, : sums.shape[1]]
    alpha = sums[:, 0:1] / sums[:, 1:2]
    here = own_ref[...]
    image = smooth_ref[...]
    for ref in image_refs:
        image = image + ref[:count, :]
    field_ref[...] = alpha * here
    residual_ref[...] = here - alpha * image


def call(kernel, outs, specs, out_specs, scratch=(), flops=0, nbytes=0, limit=small_vmem):
    return pl.pallas_call(
        kernel,
        out_shape=outs,
        in_specs=specs,
        out_specs=out_specs,
        scratch_shapes=scratch,
        compiler_params=pltpu.CompilerParams(vmem_limit_bytes=limit),
        cost_estimate=pl.CostEstimate(flops=flops, bytes_accessed=nbytes, transcendentals=0),
    )


def shape(dims, dtype=f32):
    return jax.ShapeDtypeStruct(dims, dtype)


def exchange(values, axis, step):
    return lax.ppermute(values, axis, [(i, i ^ step) for i in range(lax.axis_size(axis))])


def powers(axis):
    return [1 << i for i in range(lax.axis_size(axis).bit_length() - 1)]


def from_others(values, axis):
    count = lax.axis_size(axis)
    return [
        lax.ppermute(values, axis, [(i, (i + shift) % count) for i in range(count)]) for shift in range(1, count)
    ]


def on_device(kspace_data, coil_maps, smooth_weight, kernel_cols, kernel_rows, tile_index, caipi_cycle):
    profiles, data, weight = coil_maps[0, 0], kspace_data[0], smooth_weight[0, 0]
    coils, ny, width = profiles.shape
    nx = width // 2
    blocks = tile_index.shape[0]
    samples, ty = kernel_rows.shape
    sb = samples // blocks
    count = weight.shape[0]
    rows, groups = lax.axis_size("row"), lax.axis_size("grp")
    table = jnp.asarray(dft_table(ny))
    wide = blocks * ty
    w_shape = (blocks, 2 * sb, nx)
    row_flops = 2 * 3 * coils * wide * ny * width
    col_flops = 2 * 3 * coils * ty * blocks * (2 * sb) * width
    dma = pltpu.SemaphoreType.DMA
    x_shape = pltpu.VMEM((coils, wide, width), bf16)

    inputs = [tile_index, table, kernel_cols.T, kernel_rows.T, data, weight, profiles]
    fetched = [
        pltpu.SMEM(tile_index.shape, tile_index.dtype),
        *[pltpu.VMEM(x.shape, x.dtype) for x in inputs[1:4]],
    ]
    kept = call(
        functools.partial(tables_kernel, coils, blocks),
        [
            pltpu.VMEM(w_shape, bf16),
            pltpu.VMEM(w_shape, bf16),
            pltpu.VMEM((wide, 3 * ny), bf16),
            pltpu.VMEM((ny, 3 * wide), bf16),
            pltpu.VMEM((blocks, ty, 2 * sb), f32),
            pltpu.VMEM(profiles.shape, bf16),
            pltpu.VMEM(weight.shape, f32),
            pltpu.VMEM((2 * blocks, sb), f32),
            pltpu.VMEM(data.shape, f32),
        ],
        [pl.BlockSpec(memory_space=pltpu.SMEM)] + [HBM] * len(inputs),
        [VMEM] * 9,
        [*fetched, pltpu.VMEM((coils, ny // 2, width), bf16), dma((len(inputs) + 1,))],
        col_flops,
        limit=large_vmem,
    )(caipi_cycle, *(pltpu.with_memory_space_constraint(x, pltpu.HBM) for x in inputs))
    whigh, wlow, fwd, adj, row_weight, coil, weight, phases, data = (
        pltpu.with_memory_space_constraint(x, pltpu.VMEM) for x in kept
    )
    partial = call(
        functools.partial(rhs_kernel, coils, blocks),
        shape((ny + 8, width)),
        [VMEM] * 8,
        VMEM,
        [x_shape, x_shape],
        row_flops + col_flops,
        limit=large_vmem,
    )(phases, row_weight, whigh, wlow, adj, coil, data, weight)

    received = from_others(partial, "row")
    even_pairs = [(i, i ^ 1) for i in range(groups) if i ^ 1 < groups]
    ends = (0, groups - 1)
    beyond = [group if group in ends else ((group - 1) ^ 1) + 1 for group in range(groups)]
    odd_pairs = [
        (group * rows + row, beyond[group] * rows + ((row + 1) % rows if group in ends else row))
        for group in range(groups)
        for row in range(rows)
    ]
    beside = (("grp", even_pairs), (("grp", "row"), odd_pairs))
    weights = [lax.ppermute(weight, axes, pairs) for axes, pairs in beside]
    folded, image, mine = call(
        functools.partial(sum_kernel, ny),
        [shape((ny, width)), shape((ny, width)), shape((count, width))],
        [VMEM] * (1 + len(received)),
        [VMEM] * 3,
    )(partial, *received)
    others = [lax.ppermute(mine, axes, pairs) for axes, pairs in beside]

    predicted = call(
        functools.partial(predict_kernel, coils, blocks),
        shape((blocks, coils, 2 * sb)),
        [VMEM] * 7,
        VMEM,
        [pltpu.VMEM((blocks, 2, coils * ty, nx), bf16)] * 2,
        row_flops + col_flops,
        limit=large_vmem,
    )(phases, row_weight, folded, fwd, coil, whigh, wlow)

    predicted = [predicted, *[exchange(predicted, "band", step) for step in range(lax.axis_size("band") - 1, 0, -1)]]
    smoothed, sums = call(
        smooth_kernel,
        [shape((count, width)), shape((8, 128))],
        [VMEM] * 9,
        [VMEM, VMEM],
    )(image, mine, *others, weight, *weights, received[0], received[-1])
    sums = [sums, *[exchange(sums, "band", step) for step in range(1, lax.axis_size("band"))]]
    collapsed, squares = call(
        collapse_kernel,
        [shape(predicted[0].shape), shape((8, 128))],
        [VMEM] * len(predicted),
        [VMEM, VMEM],
    )(*predicted)
    sums = sum(sums)
    steps = powers("grp")
    for step in steps[:-1]:
        squares = squares + exchange(squares, "grp", step)
        sums = sums + exchange(sums, "grp", step)
    sums = sums + squares

    kept = call(
        functools.partial(spread_kernel, coils, blocks),
        [x_shape, x_shape],
        [VMEM] * 5,
        [VMEM] * 2,
        (),
        col_flops,
        limit=large_vmem,
    )(phases, row_weight, whigh, wlow, collapsed)
    xhigh, xlow = (pltpu.with_memory_space_constraint(x, pltpu.VMEM) for x in kept)

    def add_rows(first, last, *before):
        return call(
            functools.partial(rows_kernel, first, last),
            shape((ny, width)),
            [VMEM] * (4 + len(before)),
            VMEM,
            (),
            row_flops * (last - first) // coils,
            limit=large_vmem,
        )(adj, coil, xhigh, xlow, *before)

    unfinished = add_rows(0, coils, sums)
    sums = sums + exchange(sums, "grp", steps[-1])
    cuts = [(count, width), (count + sums.shape[0], width)] if rows == 2 else [(ny, width)]
    halves = call(
        functools.partial(cut_kernel, count if rows == 2 else ny),
        [shape(cut) for cut in cuts],
        [VMEM] * 2,
        [VMEM] * len(cuts),
        [pltpu.VMEM((ny, width), f32)],
    )(sums, unfinished)
    if rows == 2:
        images = [halves[0], exchange(halves[1], "row", 1)]
        all_sums = [sums]
    else:
        images = [lax.psum_scatter(halves[0], "row", scatter_dimension=0, tiled=True)]
        all_sums = [sums, *from_others(sums, "row")]
    solution_field, residual = call(
        functools.partial(update_kernel, len(images)),
        [shape((count, width))] * 2,
        [VMEM] * (2 + len(images) + len(all_sums)),
        [VMEM, VMEM],
    )(mine, smoothed, *images, *all_sums)
    return solution_field[None, None], residual[None, None]


def solution(mesh):
    return jax.shard_map(
        on_device,
        mesh=mesh,
        in_specs=(
            P("grp", "row", None, None),
            P("band", "grp", "row", None, None),
            P("band", "grp", "row", None),
            P(),
            P(),
            P(),
            P("band"),
        ),
        out_specs=(P("band", "grp", "row", None), P("band", "grp", "row", None)),
        check_vma=False,
    )
```

```python
import functools
import math

import jax
import jax.numpy as jnp
import ml_dtypes
import numpy as np
from jax import lax
from jax.experimental import pallas as pl
from jax.experimental.pallas import tpu as pltpu
from jax.sharding import PartitionSpec as P

reg_strength = 0.5
damping = 1.0
f32 = jnp.float32
bf16 = jnp.bfloat16
VMEM = pl.BlockSpec(memory_space=pltpu.VMEM)
HBM = pl.BlockSpec(memory_space=pltpu.HBM)
TN = (((0,), (0,)), ((), ()))
NT = (((1,), (1,)), ((), ()))
large_vmem = 20 * 1024 * 1024
small_vmem = 8 * 1024 * 1024


def dft_table(length):
    index = np.arange(length)
    angle = (index[:, None] * index[None, :] % length) * (2.0 * np.pi / length)
    parts = []
    for part in (np.cos(angle) / math.sqrt(length), -np.sin(angle) / math.sqrt(length)):
        high = part.astype(ml_dtypes.bfloat16)
        low = (part - high.astype(np.float64)).astype(ml_dtypes.bfloat16)
        parts += [high, low]
    return np.concatenate(parts, axis=0)


def split(values):
    high = values.astype(bf16)
    return high, (values - high.astype(f32)).astype(bf16)


def matmul(left, right):
    return jnp.dot(left, right, preferred_element_type=f32)


def quarter_turn(cycle, block):
    turn = lax.rem(cycle * block, 4)
    one, zero = jnp.float32(1.0), jnp.float32(0.0)
    cosine = jnp.where(turn == 0, one, zero) - jnp.where(turn == 2, one, zero)
    sine = jnp.where(turn == 1, one, zero) - jnp.where(turn == 3, one, zero)
    return cosine, sine


def phase_of(phase_ref, block):
    return phase_ref[2 * block : 2 * block + 1, :], phase_ref[2 * block + 1 : 2 * block + 2, :]


def spread(values, row_weight, whigh, wlow, xhigh, xlow, k, coils, ty):
    weighted = values[:, None, :] * row_weight[None, :, :]
    parts = split(weighted.reshape(coils * ty, values.shape[1]))
    sb = values.shape[1] // 2
    vhigh, vlow = (
        jnp.concatenate([part, jnp.concatenate([part[:, sb:], -part[:, :sb]], axis=1)], axis=0) for part in parts
    )
    rows = matmul(
        jnp.concatenate([vhigh, vlow, vhigh], axis=1),
        jnp.concatenate([whigh, whigh, wlow], axis=0),
    )
    high, low = split(rows)
    there, nx = slice(k * ty, (k + 1) * ty), rows.shape[1]
    for part in range(2):
        for c in range(coils):
            here = slice((part * coils + c) * ty, (part * coils + c + 1) * ty)
            xhigh[c, there, part * nx : (part + 1) * nx] = high[here]
            xlow[c, there, part * nx : (part + 1) * nx] = low[here]


def mirror(rows):
    left = lax.broadcasted_iota(jnp.int32, (rows, rows), 0)
    right = lax.broadcasted_iota(jnp.int32, (rows, rows), 1)
    return (lax.rem(left + right, rows) == 0).astype(f32).astype(bf16)


def mirrored(values):
    high, rest = split(values)
    low = (values - high.astype(f32) - rest.astype(f32)).astype(bf16)
    order = mirror(values.shape[0])
    return matmul(order, high) + (matmul(order, rest) + matmul(order, low))


def with_first(first, values):
    columns = values.shape[1]
    edge = lax.broadcasted_iota(jnp.int32, (8, columns), 0) == 0
    top = jnp.where(edge, first[:8], values[:8])
    return jnp.concatenate([top, values[8:]], axis=0)


def back_rows(adj, xhigh, xlow, coil, first, last):
    ny, nx = adj.shape[0], xhigh.shape[2] // 2
    half = ny // 2
    sums = [None] * 4
    for c in range(first, last):
        high, low = xhigh[c], xlow[c]
        folded = matmul(adj[...], jnp.concatenate([high, high, low], axis=0))
        even_real, even_imag = folded[:half, :nx], folded[:half, nx:]
        odd_real, odd_imag = folded[half:, :nx], folded[half:, nx:]
        lower = with_first(even_real, even_real - odd_imag), with_first(even_imag, even_imag + odd_real)
        upper = with_first(odd_real, even_real + odd_imag), with_first(odd_imag, even_imag - odd_real)
        for i, (real, imag) in enumerate((lower, upper)):
            here = slice(i * half, (i + 1) * half)
            coil_real = coil[c, here, :nx].astype(f32)
            coil_imag = coil[c, here, nx:].astype(f32)
            terms = coil_real * real + coil_imag * imag, coil_real * imag - coil_imag * real
            for j, term in enumerate(terms):
                sums[2 * i + j] = term if c == first else sums[2 * i + j] + term
    return jnp.concatenate(sums[:2], axis=1), jnp.concatenate(sums[2:], axis=1)


def tables_kernel(
    coils, blocks, cycle_ref, tile_any, table_any, cols_any, rows_any, data_any, weight_any, coil_any,
    whigh, wlow, fwd, adj, row_weight_ref, coil, weight_ref, phase_ref, data_ref,
    tile_ref, table_ref, cols_ref, rows_ref, upper, sems,
):
    ny = table_ref.shape[1]
    half = ny // 2
    ty, tx = rows_ref.shape[0], cols_ref.shape[0]
    sb = rows_ref.shape[1] // blocks
    moves = [
        (tile_any, tile_ref),
        (table_any, table_ref),
        (cols_any, cols_ref),
        (rows_any, rows_ref),
        (data_any, data_ref),
        (weight_any, weight_ref),
        (coil_any.at[:, half:, :], upper),
        (coil_any.at[:, :half, :], coil.at[:, :half, :]),
    ]
    fetches = [pltpu.make_async_copy(source, target, sems.at[i]) for i, (source, target) in enumerate(moves)]
    for fetch in fetches:
        fetch.start()
    for fetch in fetches[:-3]:
        fetch.wait()

    first = lax.broadcasted_iota(jnp.int32, (ty, half), 1) == 0
    for k in range(blocks):
        top = pl.multiple_of((tile_ref[k] // (ny // tx)) * ty, ty)
        here = slice(k * ty, (k + 1) * ty)
        for i in range(2):
            real = table_ref[pl.ds(i * ny + top, ty), :].astype(f32)
            imag = table_ref[pl.ds((2 + i) * ny + top, ty), :].astype(f32)
            odd = jnp.where(first, real[:, half:], -imag[:, :half])
            row = jnp.concatenate([real[:, :half], odd], axis=1).astype(bf16)
            for place in (0, 2) if i == 0 else (1,):
                fwd[here, place * ny : (place + 1) * ny] = row
    wide = blocks * ty
    for i in range(2):
        turned = fwd[:, i * ny : (i + 1) * ny].astype(f32).T.astype(bf16)
        for place in (0, 2) if i == 0 else (1,):
            adj[:, place * wide : (place + 1) * wide] = turned

    for k in range(blocks):
        left = pl.multiple_of(lax.rem(tile_ref[k], ny // tx) * tx, tx)
        chosen = [table_ref[pl.ds(i * ny + left, tx), :] for i in (0, 1, 2, 3)]
        stacked = jnp.concatenate(
            [jnp.concatenate([chosen[0], chosen[2]], axis=1), jnp.concatenate([chosen[1], chosen[3]], axis=1)], axis=0
        )
        here = slice(k * sb, (k + 1) * sb)
        cols = cols_ref[:, here]
        mixed = lax.dot_general(
            jnp.concatenate([cols, cols], axis=0), stacked, TN, preferred_element_type=f32
        )
        for ref, part in zip((whigh, wlow), split(mixed)):
            ref[k, :sb, :] = part[:, :ny]
            ref[k, sb:, :] = part[:, ny:]
        turned = rows_ref[:, here].astype(f32)
        row_weight = jnp.concatenate([turned, turned], axis=1)
        row_weight_ref[k] = row_weight
        for i, part in enumerate(quarter_turn(cycle_ref[0], k)):
            phase_ref[2 * k + i : 2 * k + i + 1, :] = jnp.full((1, sb), part, f32)
    for fetch in fetches[-3:-1]:
        fetch.wait()
    order = mirror(half)
    for c in range(coils):
        coil[c, half:, :] = matmul(order, upper[c]).astype(bf16)
    fetches[-1].wait()


def rhs_kernel(
    coils, blocks, phase_ref, row_weight_ref, whigh, wlow, adj, coil, data_ref, weight_ref, part_ref, xhigh, xlow
):
    ny = adj.shape[0]
    half = ny // 2
    ty = row_weight_ref.shape[1]
    sb = row_weight_ref.shape[2] // 2
    for k in range(blocks):
        here = slice(k * sb, (k + 1) * sb)
        cosine, sine = phase_of(phase_ref, k)
        real, imag = data_ref[:, 0, here], data_ref[:, 1, here]
        values = jnp.concatenate([cosine * real + sine * imag, cosine * imag - sine * real], axis=1)
        spread(values, row_weight_ref[k], whigh[k], wlow[k], xhigh, xlow, k, coils, ty)
    lower_rows, upper_rows = back_rows(adj, xhigh, xlow, coil, 0, coils)
    part_ref[:half, :] = lower_rows
    part_ref[half:ny, :] = upper_rows
    count = weight_ref.shape[0]
    edge = jnp.concatenate([weight_ref[0:1, :], weight_ref[count - 1 : count, :]], axis=0)
    edge = jnp.concatenate([edge, jnp.zeros((6, edge.shape[1]), f32)], axis=0)
    part_ref[ny:, :] = jnp.concatenate([edge, jnp.zeros_like(edge)], axis=1)


def sum_kernel(ny, *refs):
    parts, (folded_ref, image_ref, mine_ref) = refs[:-3], refs[-3:]
    total = parts[0][:ny, :]
    for part in parts[1:]:
        total = total + part[:ny, :]
    folded_ref[...] = total
    image_ref[: ny // 2, :] = total[: ny // 2]
    image_ref[ny // 2 :, :] = mirrored(total[ny // 2 :])
    count = mine_ref.shape[0]
    mine_ref[...] = image_ref[pl.ds(pl.multiple_of(lax.axis_index("row") * count, count), count), :]


def predict_kernel(
    coils, blocks, phase_ref, row_weight_ref, image_ref, fwd, coil, whigh, wlow, out_ref, thigh, tlow
):
    ny, nx = image_ref.shape[0], image_ref.shape[1] // 2
    half = ny // 2
    ty = row_weight_ref.shape[1]
    sb = row_weight_ref.shape[2] // 2
    for c in range(coils):
        products = []
        for i in range(2):
            here = slice(i * half, (i + 1) * half)
            coil_real = coil[c, here, :nx].astype(f32)
            coil_imag = coil[c, here, nx:].astype(f32)
            image_real, image_imag = image_ref[here, :nx], image_ref[here, nx:]
            products.append(coil_real * image_real - coil_imag * image_imag)
            products.append(coil_real * image_imag + coil_imag * image_real)
        lower_real, lower_imag, upper_real, upper_imag = products
        even = [with_first(lower_real, lower_real + upper_real), with_first(lower_imag, lower_imag + upper_imag)]
        odd = [with_first(upper_real, lower_imag - upper_imag), with_first(upper_imag, upper_real - lower_real)]
        folded = jnp.concatenate([jnp.concatenate(even, axis=1), jnp.concatenate(odd, axis=1)], axis=0)
        high, low = split(folded)
        grid = matmul(fwd[...], jnp.concatenate([high, high, low], axis=0))
        for ref, part in zip((thigh, tlow), split(grid)):
            ref[:, 0, c * ty : (c + 1) * ty, :] = part[:, :nx].reshape(blocks, ty, nx)
            ref[:, 1, c * ty : (c + 1) * ty, :] = part[:, nx:].reshape(blocks, ty, nx)
    for k in range(blocks):
        left_high, left_low = (ref[k].reshape(2 * coils * ty, nx) for ref in (thigh, tlow))
        right_high = whigh[k]
        mixed = lax.dot_general(
            jnp.concatenate([left_high, left_low, left_high], axis=1),
            jnp.concatenate([right_high, right_high, wlow[k]], axis=1),
            NT,
            preferred_element_type=f32,
        )
        of_real, of_imag = mixed[: coils * ty], mixed[coils * ty :]
        product = jnp.concatenate(
            [of_real[:, :sb] - of_imag[:, sb:], of_real[:, sb:] + of_imag[:, :sb]], axis=1
        )
        summed = jnp.sum(product.reshape(coils, ty, 2 * sb) * row_weight_ref[k][None, :, :], axis=1)
        real, imag = summed[:, :sb], summed[:, sb:]
        cosine, sine = phase_of(phase_ref, k)
        out_ref[k] = jnp.concatenate([cosine * real - sine * imag, sine * real + cosine * imag], axis=1)


def collapse_kernel(*refs):
    parts, (out_ref, sums_ref) = refs[:-2], refs[-2:]
    total = parts[0][...]
    for part in parts[1:]:
        total = total + part[...]
    out_ref[...] = total
    lane = lax.broadcasted_iota(jnp.int32, sums_ref.shape, 1)
    squares = jnp.sum(jnp.sum(total * total, axis=0))
    sums_ref[...] = jnp.where(lane == 1, squares, 0.0)


def spread_kernel(coils, blocks, phase_ref, row_weight_ref, whigh, wlow, collapsed_ref, xhigh, xlow):
    ty = row_weight_ref.shape[1]
    sb = row_weight_ref.shape[2] // 2
    for k in range(blocks):
        cosine, sine = phase_of(phase_ref, k)
        real, imag = collapsed_ref[k, :, :sb], collapsed_ref[k, :, sb:]
        values = jnp.concatenate([cosine * real + sine * imag, cosine * imag - sine * real], axis=1)
        spread(values, row_weight_ref[k], whigh[k], wlow[k], xhigh, xlow, k, coils, ty)


def rows_kernel(first, last, adj, coil, xhigh, xlow, *refs):
    out_ref = refs[-1]
    half = out_ref.shape[0] // 2
    for i, rows in enumerate(back_rows(adj, xhigh, xlow, coil, first, last)):
        here = slice(i * half, (i + 1) * half)
        out_ref[here, :] = rows + refs[0][here, :] if first else rows


def cut_kernel(count, sums_ref, folded_ref, *refs):
    *out_refs, whole = refs
    total = whole.shape[0]
    half = total // 2
    whole[:half, :] = folded_ref[:half, :]
    whole[half:, :] = mirrored(folded_ref[half:, :])
    for shift, out_ref in enumerate(out_refs):
        start = lax.rem(lax.axis_index("row") + shift, total // count) * count
        out_ref[:count, :] = whole[pl.ds(pl.multiple_of(start, count), count), :]
        if out_ref.shape[0] > count:
            out_ref[count:, :] = jnp.concatenate([sums_ref[...]] * (whole.shape[1] // sums_ref.shape[1]), axis=1)


def neighbours(image_ref, weight, before_ref, after_ref):
    count, nx = weight.shape
    total = image_ref.shape[0]
    place = lax.axis_index("row")
    start = place * count
    weight_up = jnp.where(place > 0, before_ref[total + 1 : total + 2, :nx], 0.0)
    weight_down = jnp.where(place < total // count - 1, after_ref[total : total + 1, :nx], 0.0)
    image_up = image_ref[pl.ds(jnp.maximum(start - 1, 0), 1), :]
    image_down = image_ref[pl.ds(jnp.minimum(start + count, total - 1), 1), :]
    row = lax.broadcasted_iota(jnp.int32, (count, nx), 0)
    column = lax.broadcasted_iota(jnp.int32, (count, nx), 1)

    def above(values, edge):
        return jnp.where(row == 0, edge, pltpu.roll(values, 1, 0))

    def below(values, edge):
        return jnp.where(row == count - 1, edge, pltpu.roll(values, count - 1, 0))

    return weight_up, weight_down, image_up, image_down, column, above, below


def smooth_kernel(
    image_ref, own_ref, odd_ref, even_ref, weight_ref, weight_odd_ref, weight_even_ref,
    before_ref, after_ref, out_ref, sums_ref,
):
    nx = image_ref.shape[1] // 2
    weight, weight_even = weight_ref[...], weight_even_ref[...]
    group = lax.axis_index("grp")
    inside = jnp.logical_and(group > 0, group < lax.axis_size("grp") - 1)
    weight_odd = jnp.where(inside, weight_odd_ref[...], 0.0)
    weight_up, weight_down, image_up, image_down, column, above, below = neighbours(
        image_ref, weight, before_ref, after_ref
    )
    weight_left = jnp.where(column == 0, 0.0, pltpu.roll(weight, 1, 1))
    weight_right = jnp.where(column == nx - 1, 0.0, pltpu.roll(weight, nx - 1, 1))
    weight_above, weight_below = above(weight, weight_up), below(weight, weight_down)
    squares = curvature = 0.0
    for part in range(2):
        lanes = slice(part * nx, (part + 1) * nx)
        here = own_ref[:, lanes]
        flux = weight_even * (here - even_ref[:, lanes]) + weight_odd * (here - odd_ref[:, lanes])
        flux += weight_above * (here - above(here, image_up[:, lanes]))
        flux += weight_below * (here - below(here, image_down[:, lanes]))
        flux += weight_left * (here - pltpu.roll(here, 1, 1))
        flux += weight_right * (here - pltpu.roll(here, nx - 1, 1))
        result = reg_strength * (weight * flux) + damping * here
        out_ref[:, lanes] = result
        squares += here * here
        curvature += here * result
    norm, energy = jnp.sum(squares), jnp.sum(curvature)
    lane = lax.broadcasted_iota(jnp.int32, sums_ref.shape, 1)
    sums_ref[...] = jnp.where(lane == 0, norm, jnp.where(lane == 1, energy, 0.0))


def update_kernel(images, own_ref, smooth_ref, *refs):
    image_refs, sums_refs, (field_ref, residual_ref) = refs[:images], refs[images:-2], refs[-2:]
    count = smooth_ref.shape[0]
    sums = sums_refs[0][0:1, :]
    for ref in sums_refs[1:]:
        sums = sums + ref[0:1, :]
    for ref in image_refs:
        if ref.shape[0] > count:
            sums = sums + ref[count : count + 1, : sums.shape[1]]
    alpha = sums[:, 0:1] / sums[:, 1:2]
    here = own_ref[...]
    image = smooth_ref[...]
    for ref in image_refs:
        image = image + ref[:count, :]
    field_ref[...] = alpha * here
    residual_ref[...] = here - alpha * image


def call(kernel, outs, specs, out_specs, scratch=(), flops=0, nbytes=0, limit=small_vmem):
    return pl.pallas_call(
        kernel,
        out_shape=outs,
        in_specs=specs,
        out_specs=out_specs,
        scratch_shapes=scratch,
        compiler_params=pltpu.CompilerParams(vmem_limit_bytes=limit),
        cost_estimate=pl.CostEstimate(flops=flops, bytes_accessed=nbytes, transcendentals=0),
    )


def shape(dims, dtype=f32):
    return jax.ShapeDtypeStruct(dims, dtype)


def exchange(values, axis, step):
    return lax.ppermute(values, axis, [(i, i ^ step) for i in range(lax.axis_size(axis))])


def powers(axis):
    return [1 << i for i in range(lax.axis_size(axis).bit_length() - 1)]


def from_others(values, axis):
    count = lax.axis_size(axis)
    return [
        lax.ppermute(values, axis, [(i, (i + shift) % count) for i in range(count)]) for shift in range(1, count)
    ]


def on_device(kspace_data, coil_maps, smooth_weight, kernel_cols, kernel_rows, tile_index, caipi_cycle):
    profiles, data, weight = coil_maps[0, 0], kspace_data[0], smooth_weight[0, 0]
    coils, ny, width = profiles.shape
    nx = width // 2
    blocks = tile_index.shape[0]
    samples, ty = kernel_rows.shape
    sb = samples // blocks
    count = weight.shape[0]
    rows, groups = lax.axis_size("row"), lax.axis_size("grp")
    table = jnp.asarray(dft_table(ny))
    wide = blocks * ty
    w_shape = (blocks, 2 * sb, nx)
    row_flops = 2 * 3 * coils * wide * ny * width
    col_flops = 2 * 3 * coils * ty * blocks * (2 * sb) * width
    dma = pltpu.SemaphoreType.DMA
    x_shape = pltpu.VMEM((coils, wide, width), bf16)

    inputs = [tile_index, table, kernel_cols.T, kernel_rows.T, data, weight, profiles]
    fetched = [
        pltpu.SMEM(tile_index.shape, tile_index.dtype),
        *[pltpu.VMEM(x.shape, x.dtype) for x in inputs[1:4]],
    ]
    kept = call(
        functools.partial(tables_kernel, coils, blocks),
        [
            pltpu.VMEM(w_shape, bf16),
            pltpu.VMEM(w_shape, bf16),
            pltpu.VMEM((wide, 3 * ny), bf16),
            pltpu.VMEM((ny, 3 * wide), bf16),
            pltpu.VMEM((blocks, ty, 2 * sb), f32),
            pltpu.VMEM(profiles.shape, bf16),
            pltpu.VMEM(weight.shape, f32),
            pltpu.VMEM((2 * blocks, sb), f32),
            pltpu.VMEM(data.shape, f32),
        ],
        [pl.BlockSpec(memory_space=pltpu.SMEM)] + [HBM] * len(inputs),
        [VMEM] * 9,
        [*fetched, pltpu.VMEM((coils, ny // 2, width), bf16), dma((len(inputs) + 1,))],
        col_flops,
        limit=large_vmem,
    )(caipi_cycle, *(pltpu.with_memory_space_constraint(x, pltpu.HBM) for x in inputs))
    whigh, wlow, fwd, adj, row_weight, coil, weight, phases, data = (
        pltpu.with_memory_space_constraint(x, pltpu.VMEM) for x in kept
    )
    partial = call(
        functools.partial(rhs_kernel, coils, blocks),
        shape((ny + 8, width)),
        [VMEM] * 8,
        VMEM,
        [x_shape, x_shape],
        row_flops + col_flops,
        limit=large_vmem,
    )(phases, row_weight, whigh, wlow, adj, coil, data, weight)

    received = from_others(partial, "row")
    even_pairs = [(i, i ^ 1) for i in range(groups) if i ^ 1 < groups]
    ends = (0, groups - 1)
    beyond = [group if group in ends else ((group - 1) ^ 1) + 1 for group in range(groups)]
    odd_pairs = [
        (group * rows + row, beyond[group] * rows + ((row + 1) % rows if group in ends else row))
        for group in range(groups)
        for row in range(rows)
    ]
    beside = (("grp", even_pairs), (("grp", "row"), odd_pairs))
    weights = [lax.ppermute(weight, axes, pairs) for axes, pairs in beside]
    folded, image, mine = call(
        functools.partial(sum_kernel, ny),
        [shape((ny, width)), shape((ny, width)), shape((count, width))],
        [VMEM] * (1 + len(received)),
        [VMEM] * 3,
    )(partial, *received)
    others = [lax.ppermute(mine, axes, pairs) for axes, pairs in beside]

    predicted = call(
        functools.partial(predict_kernel, coils, blocks),
        shape((blocks, coils, 2 * sb)),
        [VMEM] * 7,
        VMEM,
        [pltpu.VMEM((blocks, 2, coils * ty, nx), bf16)] * 2,
        row_flops + col_flops,
        limit=large_vmem,
    )(phases, row_weight, folded, fwd, coil, whigh, wlow)

    predicted = [predicted, *[exchange(predicted, "band", step) for step in range(lax.axis_size("band") - 1, 0, -1)]]
    smoothed, sums = call(
        smooth_kernel,
        [shape((count, width)), shape((8, 128))],
        [VMEM] * 9,
        [VMEM, VMEM],
    )(image, mine, *others[::-1], weight, *weights[::-1], received[0], received[-1])
    sums = [sums, *[exchange(sums, "band", step) for step in range(1, lax.axis_size("band"))]]
    collapsed, squares = call(
        collapse_kernel,
        [shape(predicted[0].shape), shape((8, 128))],
        [VMEM] * len(predicted),
        [VMEM, VMEM],
    )(*predicted)
    sums = sum(sums)
    steps = powers("grp")
    for step in steps[:-1]:
        squares = squares + exchange(squares, "grp", step)
        sums = sums + exchange(sums, "grp", step)
    sums = sums + squares

    kept = call(
        functools.partial(spread_kernel, coils, blocks),
        [x_shape, x_shape],
        [VMEM] * 5,
        [VMEM] * 2,
        (),
        col_flops,
        limit=large_vmem,
    )(phases, row_weight, whigh, wlow, collapsed)
    xhigh, xlow = (pltpu.with_memory_space_constraint(x, pltpu.VMEM) for x in kept)

    def add_rows(first, last, *before):
        return call(
            functools.partial(rows_kernel, first, last),
            shape((ny, width)),
            [VMEM] * (4 + len(before)),
            VMEM,
            (),
            row_flops * (last - first) // coils,
            limit=large_vmem,
        )(adj, coil, xhigh, xlow, *before)

    unfinished = add_rows(0, coils, sums)
    sums = sums + exchange(sums, "grp", steps[-1])
    cuts = [(count, width), (count + sums.shape[0], width)] if rows == 2 else [(ny, width)]
    halves = call(
        functools.partial(cut_kernel, count if rows == 2 else ny),
        [shape(cut) for cut in cuts],
        [VMEM] * 2,
        [VMEM] * len(cuts),
        [pltpu.VMEM((ny, width), f32)],
    )(sums, unfinished)
    if rows == 2:
        images = [halves[0], exchange(halves[1], "row", 1)]
        all_sums = [sums]
    else:
        images = [lax.psum_scatter(halves[0], "row", scatter_dimension=0, tiled=True)]
        all_sums = [sums, *from_others(sums, "row")]
    solution_field, residual = call(
        functools.partial(update_kernel, len(images)),
        [shape((count, width))] * 2,
        [VMEM] * (2 + len(images) + len(all_sums)),
        [VMEM, VMEM],
    )(mine, smoothed, *images, *all_sums)
    return solution_field[None, None], residual[None, None]


def solution(mesh):
    return jax.shard_map(
        on_device,
        mesh=mesh,
        in_specs=(
            P("grp", "row", None, None),
            P("band", "grp", "row", None, None),
            P("band", "grp", "row", None),
            P(),
            P(),
            P(),
            P("band"),
        ),
        out_specs=(P("band", "grp", "row", None), P("band", "grp", "row", None)),
        check_vma=False,
    )
```
